256 devices in a mesh: sp: 8 (over z), gx: 32 (over y, x, core).
Axes of the slice: x: 4, y: 4, z: 8, core: 2. Of those that a mesh axis runs over, the one named last changes fastest.
Arguments:
- tensor: float32 [64, 512, 6144], P('sp', 'gx'), may hold values from -32 to 32
- start_species: float32 [64, 16], replicated, may hold values from -4 to 4
- start_plane: float32 [512, 128], replicated, may hold values from -4 to 4
Outputs:
- core_block: float32 [6144, 16, 128], P(('sp', 'gx'))
- block_peaks: float32 [6144, 16], P(('sp', 'gx'))
The draws below stay inside these ranges and needn't reach their ends.
All inputs are finite; a program needn't handle non-finite values.
Results may differ from the reference program's by a relative error of at most 0.0003.
Values sent between devices are 32-bit elements; how exact they have to be, the bound alone decides.
No kernel may reach another device: no remote copies, remote signals or barrier semaphores. Data moves between devices by JAX's collectives and lax.ppermute only.
A program may use at most 128 MiB of HBM per device.

```python
import math
import jax
import jax.numpy as jnp
from jax import lax

S = 64
NX = 512
R1 = 16
R2 = 128
SWEEPS = 4
CELLS = 6144


def draw_tensor(key, part):
    key = jax.random.fold_in(key, 11)
    key_species, key_rows, key_noise = jax.random.split(key, 3)
    species_scale = jnp.exp(jax.random.uniform(key_species, (S, 1, 1), jnp.float32, math.log(0.25), math.log(4.0)))
    row_scale = jnp.exp(jax.random.uniform(key_rows, (1, NX, 1), jnp.float32, math.log(0.5), math.log(2.0)))
    noise = jax.random.truncated_normal(key_noise, -4.0, 4.0, (S, NX, CELLS), jnp.float32)
    return (species_scale * row_scale * noise).astype(jnp.float32)


def scatter_about(stream_key, shape, spread, most, held_as=jnp.bfloat16):
    drawn = jax.random.normal(stream_key, shape, jnp.float32) * spread
    return jnp.minimum(jnp.maximum(drawn, -most), most).astype(held_as)


def setup_inputs(seed: int = 0) -> dict:
    splits = jax.random.split(jax.random.key(seed), 4)
    return {
        "tensor": draw_tensor(jax.random.fold_in(splits[3], 71), 0),
        "start_species": scatter_about(splits[1], (S, R1), 1.0, 4.0, jnp.float32),
        "start_plane": scatter_about(splits[2], (NX, R2), 1.0, 4.0, jnp.float32),
    }


def subspace(gram, start):
    basis = start
    for _ in range(SWEEPS):
        image_block = jnp.dot(gram, basis, precision=lax.Precision.HIGHEST)
        inner_gram = jnp.dot(image_block.T, image_block, precision=lax.Precision.HIGHEST)
        factor_low = jnp.linalg.cholesky(inner_gram)
        basis = lax.linalg.triangular_solve(factor_low, image_block, left_side=False, lower=True, transpose_a=True)
    return basis

def reference(tensor, start_species, start_plane):
    flattened = tensor.reshape(tensor.shape[0], -1)
    gram_species = jnp.dot(flattened, flattened.T, precision=lax.Precision.HIGHEST)
    basis_species = subspace(gram_species, start_species)
    reduced = jnp.einsum('sxc,sr->xcr', tensor, basis_species, precision=lax.Precision.HIGHEST)
    plane_flat = reduced.reshape(reduced.shape[0], -1)
    gram_plane = jnp.dot(plane_flat, plane_flat.T, precision=lax.Precision.HIGHEST)
    basis_plane = subspace(gram_plane, start_plane)
    core_block = jnp.einsum('xcr,xq->crq', reduced, basis_plane, precision=lax.Precision.HIGHEST)
    block_peaks = jnp.max(jnp.abs(core_block), axis=2)
    return (core_block, block_peaks)
```

```python
import jax
import jax.numpy as jnp
from jax import lax
from jax.experimental import pallas as pl
from jax.experimental.pallas import tpu as pltpu
from jax.sharding import PartitionSpec as P

SWEEPS = 4
F32 = jnp.float32
BF16 = jnp.bfloat16
BOTH = ("sp", "gx")
NN = (((1,), (0,)), ((), ()))
NT = (((1,), (1,)), ((), ()))
TN = (((0,), (0,)), ((), ()))
PARAMS = pltpu.CompilerParams(vmem_limit_bytes=48 * 1024 * 1024)


def exact_dot(a, b, dims=NN):
    return lax.dot_general(a, b, dims, precision=lax.Precision.HIGHEST, preferred_element_type=F32)


def bf16_dot(a, b, dims=NN):
    return lax.dot_general(a, b, dims, preferred_element_type=F32)


def split2(x):
    high = x.astype(BF16)
    return high, (x - high.astype(F32)).astype(BF16)


def spread(x, i, j):
    return jnp.broadcast_to(x[i : i + 1, j : j + 1], (8, 128))


def inverse_factor(panels, count):
    sub = lax.broadcasted_iota(jnp.int32, (8, 128), 0)
    lane = lax.broadcasted_iota(jnp.int32, (8, 128), 1)
    grams = list(panels)
    extra = [jnp.where(lane == sub + 8 * p, 1.0, 0.0).astype(F32) for p in range(count)]
    result = []
    for p in range(count):
        panel, tail = grams[p], extra[p]
        cell = [[None] * 8 for _ in range(8)]
        for i in range(8):
            for j in range(i + 1):
                cell[i][j] = spread(panel, i, 8 * p + j)
        pivots, mults = [], []
        for j in range(8):
            at = lambda i, k: cell[i][k] if i >= k else cell[k][i]
            recip = 1.0 / cell[j][j]
            pivots.append(recip)
            scaled = [None if i == j else at(i, j) * recip for i in range(8)]
            mults.append(scaled)
            fresh = [[None] * 8 for _ in range(8)]
            for i in range(8):
                for k in range(i + 1):
                    if i == j and k == j:
                        fresh[i][k] = -recip
                    elif i == j:
                        fresh[i][k] = scaled[k]
                    elif k == j:
                        fresh[i][k] = scaled[i]
                    else:
                        fresh[i][k] = cell[i][k] - scaled[i] * at(k, j)
            cell = fresh
        inverse = lambda i, k: cell[i][k] if i >= k else cell[k][i]
        rows = tail
        for j in range(8):
            column = jnp.zeros((8, 128), F32)
            for i in range(j + 1, 8):
                column = jnp.where(sub == i, mults[j][i], column)
            rows = rows - column * rows[j : j + 1, :]
        root = jnp.zeros((8, 128), F32)
        for j in range(8):
            root = jnp.where(sub == j, pivots[j], root)
        result.append(rows * jnp.sqrt(root))
        if p + 1 == count:
            break
        solved_gram, solved_tail = None, None
        for j in range(8):
            column = -inverse(0, j)
            for i in range(1, 8):
                column = jnp.where(sub == i, -inverse(i, j), column)
            a, b = column * panel[j : j + 1, :], column * tail[j : j + 1, :]
            solved_gram = a if j == 0 else solved_gram + a
            solved_tail = b if j == 0 else solved_tail + b
        for k in range(p + 1, count):
            for j in range(8):
                factor = jnp.broadcast_to(grams[k][:, 8 * p + j : 8 * p + j + 1], (8, 128))
                if j == 0:
                    da, db = factor * solved_gram[0:1, :], factor * solved_tail[0:1, :]
                else:
                    da = da + factor * solved_gram[j : j + 1, :]
                    db = db + factor * solved_tail[j : j + 1, :]
            grams[k] = grams[k] - da
            extra[k] = extra[k] - db
    return result


def subspace(gram, start):
    basis = start
    for _ in range(SWEEPS):
        image_block = exact_dot(gram, basis)
        inner = exact_dot(image_block, image_block, TN)
        panels = [inner[8 * p : 8 * p + 8, :] for p in range(inner.shape[0] // 8)]
        factor = jnp.concatenate(inverse_factor(panels, len(panels)), axis=0)
        basis = exact_dot(image_block, factor, NT)
    return basis


def subspace_narrow(gram, start):
    basis = start
    for _ in range(SWEEPS):
        image_block = exact_dot(gram, basis)
        inner = exact_dot(image_block, image_block, TN)
        panels = [inner[8 * p : 8 * p + 8, :] for p in range(2)]
        factor = jnp.concatenate(inverse_factor(panels, 2) + [jnp.zeros((112, 128), F32)], axis=0)
        basis = exact_dot(image_block, factor, NT)
    return basis


def cells_first_kernel(x_ref, o_ref, tile_ref):
    for k in range(x_ref.shape[1] // 128):
        lanes = slice(128 * k, 128 * (k + 1))
        tile_ref[k] = x_ref[:, lanes]
        rows = jnp.concatenate([tile_ref[k, pl.ds(x, 8, stride=16), :] for x in range(16)], axis=0)
        o_ref[lanes, :] = rows.T


def cells_first(block):
    cells = block.shape[2]
    step = 768
    return pl.pallas_call(
        cells_first_kernel,
        out_shape=jax.ShapeDtypeStruct((cells, 128), F32),
        grid=(cells // step,),
        in_specs=[pl.BlockSpec((128, step), lambda i: (0, i))],
        out_specs=pl.BlockSpec((step, 128), lambda i: (i, 0)),
        scratch_shapes=[pltpu.VMEM((step // 128, 128, 128), F32)],
        compiler_params=PARAMS,
    )(block.reshape(128, cells))


def species_gram_kernel(r_ref, o_ref, ht_ref, h_ref, l_ref):
    for s in range(8):
        high, low = split2(r_ref[s])
        ht_ref[128 * s : 128 * (s + 1), :] = r_ref[s].T.astype(BF16)
        h_ref[:, 128 * s : 128 * (s + 1)] = high
        l_ref[:, 128 * s : 128 * (s + 1)] = low
    lane = lax.broadcasted_iota(jnp.int32, (8, 256), 1) % 128
    rows = []
    for a in range(4):
        left = ht_ref[256 * a : 256 * (a + 1), :]
        parts = [[], []]
        for b in range(4):
            right = slice(256 * b, 256 * (b + 1))
            prod = bf16_dot(left, l_ref[:, right])
            if b >= a:
                main = bf16_dot(left, h_ref[:, right])
                prod = prod + (main if b > a else 0.5 * main)
            for half in range(2):
                acc = prod[128 * half : 128 * half + 8]
                for x in range(1, 16):
                    acc = jnp.where(lane // 8 == x, prod[128 * half + 8 * x : 128 * half + 8 * x + 8], acc)
                parts[half].append(acc)
        for half in range(2):
            rows.append(jnp.concatenate(parts[half], axis=1))
    wide = jnp.concatenate(rows, axis=0)
    fold = jnp.where(
        lax.broadcasted_iota(jnp.int32, (1024, 64), 0) // 128 * 8
        + lax.broadcasted_iota(jnp.int32, (1024, 64), 0) % 8
        == lax.broadcasted_iota(jnp.int32, (1024, 64), 1),
        1.0,
        0.0,
    ).astype(F32)
    half = exact_dot(wide, fold)
    gram = half + half.T
    o_ref[...] = jnp.concatenate([gram[0:32], gram[32:64]], axis=1)


def species_gram(received):
    return pl.pallas_call(
        species_gram_kernel,
        out_shape=jax.ShapeDtypeStruct((32, 128), F32),
        scratch_shapes=[
            pltpu.VMEM((1024, 768), BF16),
            pltpu.VMEM((768, 1024), BF16),
            pltpu.VMEM((768, 1024), BF16),
        ],
        compiler_params=PARAMS,
    )(received)


def plane_gram_kernel(r_ref, g_ref, start_ref, turned_ref, o_ref, wh_ref, wl_ref, red_ref):
    folded = jnp.sum(g_ref[...], axis=0)
    gram = jnp.concatenate([folded[:, 0:64], folded[:, 64:128]], axis=0)
    start = jnp.concatenate([start_ref[...], jnp.zeros((64, 112), F32)], axis=1)
    basis = subspace_narrow(gram, start)[:, 0:16]
    widen = jnp.where(
        lax.broadcasted_iota(jnp.int32, (16, 256), 1) // 16 == lax.broadcasted_iota(jnp.int32, (16, 256), 0), 1.0, 0.0
    ).astype(F32)
    wide = exact_dot(basis, widen)
    keep = (
        lax.broadcasted_iota(jnp.int32, (128, 256), 0) // 8 == lax.broadcasted_iota(jnp.int32, (128, 256), 1) % 16
    )
    for s in range(8):
        weights = jnp.where(keep, jnp.concatenate([wide[8 * s : 8 * s + 8]] * 16, axis=0), 0.0)
        high, low = split2(weights)
        wh_ref[128 * s : 128 * (s + 1), :] = high
        wl_ref[128 * s : 128 * (s + 1), :] = low
    total = None
    for s in range(8):
        high, low = split2(r_ref[s])
        rows = slice(128 * s, 128 * (s + 1))
        term = bf16_dot(high, wh_ref[rows]) + bf16_dot(high, wl_ref[rows]) + bf16_dot(low, wh_ref[rows])
        total = term if s == 0 else total + term
    red_ref[...] = total
    lane = lax.broadcasted_iota(jnp.int32, (16, 128), 1)
    blank = jnp.zeros((8, 256), F32)
    for a in range(8):
        rows = []
        for b in range(4):
            g = 4 * a + b
            rows += [red_ref[24 * g : 24 * g + 24, :], blank]
        turned = jnp.concatenate(rows, axis=0).T
        shifted = [turned] + [pltpu.roll(turned, 32 * k, 1) for k in range(1, 4)]
        for b in range(4):
            g = 4 * a + b
            for quad in range(4):
                block = None
                for k in range(4):
                    r = 4 * quad + k
                    piece = shifted[(k - b) % 4][16 * r : 16 * r + 16, :]
                    block = piece if k == 0 else jnp.where(lane // 32 == k, piece, block)
                turned_ref[16 * g : 16 * g + 16, 128 * quad : 128 * (quad + 1)] = block
    high, low = split2(turned_ref[...])
    left = jnp.concatenate([high, high, low], axis=1)
    right = jnp.concatenate([high, low, high], axis=1)
    at = 0
    for i in range(4):
        for j in range(i, 4):
            o_ref[at : at + 128, :] = bf16_dot(left[128 * i : 128 * (i + 1)], right[128 * j : 128 * (j + 1)], NT)
            at += 128


def plane_gram(received, grams, start_species):
    return pl.pallas_call(
        plane_gram_kernel,
        out_shape=(jax.ShapeDtypeStruct((512, 512), F32), jax.ShapeDtypeStruct((1280, 128), F32)),
        scratch_shapes=[pltpu.VMEM((1024, 256), BF16), pltpu.VMEM((1024, 256), BF16), pltpu.VMEM((768, 256), F32)],
        compiler_params=PARAMS,
    )(received, grams, start_species)


def core_kernel(packed_ref, turned_ref, start_ref, core_ref):
    blocks = {}
    at = 0
    for i in range(4):
        for j in range(i, 4):
            blocks[i, j] = packed_ref[at : at + 128, :]
            if i != j:
                blocks[j, i] = blocks[i, j].T
            at += 128
    gram = jnp.concatenate(
        [jnp.concatenate([blocks[i, j] for j in range(4)], axis=1) for i in range(4)], axis=0
    )
    basis = subspace(gram, start_ref[...])
    th, tl = split2(turned_ref[...].T)
    bh, bl = split2(basis)
    core = bf16_dot(th, bh) + bf16_dot(th, bl) + bf16_dot(tl, bh)
    for r in range(16):
        core_ref[pl.ds(r, 24, stride=16), :] = core[32 * r : 32 * r + 24, :]


def core_of(packed, turned, start_plane):
    return pl.pallas_call(
        core_kernel,
        out_shape=jax.ShapeDtypeStruct((384, 128), F32),
        compiler_params=PARAMS,
    )(packed, turned, start_plane)


def gathered(x, axis, count):
    copies = jnp.broadcast_to(x[None], (count,) + x.shape)
    return lax.all_to_all(copies, axis, 0, 0, tiled=True)


def per_device(tensor, start_species, start_plane):
    sent = cells_first(tensor).reshape(256, 24, 128)
    received = lax.all_to_all(sent, BOTH, 0, 0, tiled=True).reshape(8, 768, 128)
    partial_species = species_gram(received)
    partial_species = jnp.sum(gathered(partial_species, "gx", 32), axis=0)
    turned, partial_plane = plane_gram(received, gathered(partial_species, "sp", 8), start_species)
    share = jnp.sum(lax.all_to_all(partial_plane.reshape(32, 40, 128), "gx", 0, 0, tiled=True), axis=0)
    share = jnp.sum(gathered(share, "sp", 8), axis=0)
    packed = gathered(share, "gx", 32).reshape(1280, 128)
    core_block = core_of(packed, turned, start_plane).reshape(24, 16, 128)
    return core_block, jnp.max(jnp.abs(core_block), axis=2)


def solution(mesh):
    placed = (P("sp", "gx", None), P(), P())
    return jax.shard_map(
        per_device,
        mesh=mesh,
        in_specs=placed,
        out_specs=(P(BOTH, None, None), P(BOTH, None)),
        check_vma=False,
    )
```

```python
import jax
import jax.numpy as jnp
from jax import lax
from jax.experimental import pallas as pl
from jax.experimental.pallas import tpu as pltpu
from jax.sharding import PartitionSpec as P

SWEEPS = 4
HEIGHT = 2
F32 = jnp.float32
BF16 = jnp.bfloat16
BOTH = ("sp", "gx")
NN = (((1,), (0,)), ((), ()))
NT = (((1,), (1,)), ((), ()))
TN = (((0,), (0,)), ((), ()))
PAIR = [(d, d ^ 1) for d in range(32)]
PLANES = [[d + core for d in range(0, 32, 2)] for core in range(2)]


def grant(mebibytes):
    return pltpu.CompilerParams(vmem_limit_bytes=mebibytes * 1024 * 1024)


def exact_dot(a, b, dims=NN):
    return lax.dot_general(a, b, dims, precision=lax.Precision.HIGHEST, preferred_element_type=F32)


def bf16_dot(a, b, dims=NN):
    return lax.dot_general(a, b, dims, preferred_element_type=F32)


def split2(x):
    high = x.astype(BF16)
    return high, (x - high.astype(F32)).astype(BF16)


def split3(x):
    high = x.astype(BF16)
    rest = x - high.astype(F32)
    mid = rest.astype(BF16)
    return high, mid, (rest - mid.astype(F32)).astype(BF16)


def six(a, b, dims=NN):
    (ah, am, al), (bh, bm, bl) = a, b
    ka, kb = dims[0][0][0], dims[0][1][0]
    left = jnp.concatenate([ah, ah, am, ah, al, am], axis=ka)
    right = jnp.concatenate([bh, bm, bh, bl, bh, bm], axis=kb)
    return bf16_dot(left, right, dims)


def across(x, j):
    return jnp.broadcast_to(x[:, j : j + 1], (8, 128))


def full_row(x, i):
    return jnp.broadcast_to(x[i : i + 1, :], (8, 128))


def inverse_factor(panels, height=1, between=None):
    count = len(panels)
    sub = lax.broadcasted_iota(jnp.int32, (8, 128), 0)
    lane = lax.broadcasted_iota(jnp.int32, (8, 128), 1)
    state = list(panels)
    result = []
    for p in range(0, count, height):
        width = 8 * height
        own = (lane >= 8 * p) & (lane < 8 * p + width)
        cols = [[across(state[p + t], 8 * p + j) for t in range(height)] for j in range(width)]
        solved = [
            jnp.where(own, jnp.where(lane == sub + 8 * (p + t), 1.0, 0.0), state[p + t]) for t in range(height)
        ]
        rows = [jnp.where(lane < 8 * p + width, x, 0.0) for x in solved]
        root = [None] * height
        diag = full_row(cols[0][0], 0)
        for j in range(width):
            tj, ij = divmod(j, 8)
            recip = 1.0 / diag
            pivots = [full_row(cols[k][tj], ij) for k in range(j + 1, width)]
            if j + 1 < width:
                tn, i_n = divmod(j + 1, 8)
                diag = full_row(cols[j + 1][tn], i_n) - (full_row(cols[j][tn], i_n) * pivots[0]) * recip
            root[tj] = recip if ij == 0 else jnp.where(sub == ij, recip, root[tj])
            mult = []
            for t in range(height):
                m = cols[j][t] * recip
                mult.append(jnp.where(sub == ij, 0.0, m) if t == tj else m)
            for k in range(j + 1, width):
                cols[k] = [cols[k][t] - mult[t] * pivots[k - j - 1] for t in range(height)]
            pivot = full_row(solved[tj], ij)
            solved = [solved[t] - mult[t] * pivot for t in range(height)]
            pivot = full_row(rows[tj], ij)
            for t in range(tj, height):
                m = jnp.where(sub > ij, mult[t], 0.0) if t == tj else mult[t]
                rows[t] = rows[t] - m * pivot
        for t in range(height):
            result.append(rows[t] * jnp.sqrt(root[t]))
            solved[t] = solved[t] * root[t]
        near = min(p + 2 * height, count)
        for k in range(p + height, near):
            fresh = jnp.where(own, 0.0, state[k])
            for j in range(width):
                tj, ij = divmod(j, 8)
                fresh = fresh - across(state[k], 8 * p + j) * full_row(solved[tj], ij)
            state[k] = fresh
        if near < count:
            far = jnp.concatenate(state[near:], axis=0)
            ends = [jnp.zeros((8 * n, 128), F32) for n in (p, 16 - p - height)]
            weights = jnp.concatenate(([ends[0]] if p else []) + solved + [ends[1]], axis=0)
            change = six(split3(far), split3(weights))
            for k in range(near, count):
                at = 8 * (k - near)
                state[k] = jnp.where(own, 0.0, state[k]) - change[at : at + 8]
        if between is not None:
            between(p // height)
    return result


def subspace(gram, start, image_ref):
    split_gram = split3(gram)
    image_block = six(split_gram, split3(start))
    for sweep in range(SWEEPS):
        pieces = split3(image_block)
        inner = six(pieces, pieces, TN)
        step = 8 * HEIGHT

        def ahead(panel):
            rows = slice(4 * step * panel, 4 * step * (panel + 1))
            image_ref[rows, :] = six(tuple(g[rows] for g in split_gram), pieces)

        last = sweep + 1 == SWEEPS
        tiles = [inner[8 * p : 8 * p + 8] for p in range(16)]
        factor = split3(jnp.concatenate(inverse_factor(tiles, HEIGHT, None if last else ahead), axis=0))
        image_block = six(pieces if last else split3(image_ref[...]), factor, NT)
    return image_block


def subspace_narrow(gram, start):
    split_gram = split3(gram)
    image_block = six(split_gram, split3(start))
    blank = jnp.zeros((112, 128), F32)
    for sweep in range(SWEEPS):
        pieces = split3(image_block)
        inner = six(pieces, pieces, TN)
        ahead = pieces if sweep + 1 == SWEEPS else split3(six(split_gram, pieces))
        factor = inverse_factor([inner[0:8], inner[8:16]], 2)
        image_block = six(ahead, split3(jnp.concatenate(factor + [blank], axis=0)), NT)
    return image_block


def cells_first_kernel(x_ref, o_ref, tile_ref):
    for k in range(x_ref.shape[1] // 128):
        lanes = slice(128 * k, 128 * (k + 1))
        tile_ref[k] = x_ref[:, lanes]
        rows = jnp.concatenate([tile_ref[k, pl.ds(x, 8, stride=16), :] for x in range(16)], axis=0)
        o_ref[lanes, :] = rows.T


def cells_first(block):
    cells = block.shape[2]
    step = 768
    return pl.pallas_call(
        cells_first_kernel,
        out_shape=jax.ShapeDtypeStruct((cells, 128), F32),
        grid=(cells // step,),
        in_specs=[pl.BlockSpec((128, step), lambda i: (0, i))],
        out_specs=pl.BlockSpec((step, 128), lambda i: (i, 0)),
        scratch_shapes=[pltpu.VMEM((step // 128, 128, 128), F32)],
        compiler_params=grant(8),
    )(block.reshape(128, cells))


def species_gram_kernel(r_ref, o_ref, ht_ref, h_ref, l_ref):
    for s in range(8):
        high, low = split2(r_ref[s])
        ht_ref[128 * s : 128 * (s + 1), :] = r_ref[s].T.astype(BF16)
        h_ref[:, 128 * s : 128 * (s + 1)] = high
        l_ref[:, 128 * s : 128 * (s + 1)] = low
    lane = lax.broadcasted_iota(jnp.int32, (8, 256), 1) % 128
    rows = []
    for a in range(4):
        left = ht_ref[256 * a : 256 * (a + 1), :]
        parts = [[], []]
        for b in range(4):
            right = slice(256 * b, 256 * (b + 1))
            prod = bf16_dot(left, l_ref[:, right])
            if b >= a:
                main = bf16_dot(left, h_ref[:, right])
                prod = prod + (main if b > a else 0.5 * main)
            for half in range(2):
                acc = prod[128 * half : 128 * half + 8]
                for x in range(1, 16):
                    acc = jnp.where(lane // 8 == x, prod[128 * half + 8 * x : 128 * half + 8 * x + 8], acc)
                parts[half].append(acc)
        for half in range(2):
            rows.append(jnp.concatenate(parts[half], axis=1))
    wide = jnp.concatenate(rows, axis=0)
    fold = jnp.where(
        lax.broadcasted_iota(jnp.int32, (1024, 64), 0) // 128 * 8
        + lax.broadcasted_iota(jnp.int32, (1024, 64), 0) % 8
        == lax.broadcasted_iota(jnp.int32, (1024, 64), 1),
        1.0,
        0.0,
    ).astype(F32)
    half = exact_dot(wide, fold)
    gram = half + half.T
    o_ref[...] = jnp.concatenate([gram[0:32], gram[32:64]], axis=1)


def species_gram(received):
    return pl.pallas_call(
        species_gram_kernel,
        out_shape=jax.ShapeDtypeStruct((32, 128), F32),
        scratch_shapes=[
            pltpu.VMEM((1024, 768), BF16),
            pltpu.VMEM((768, 1024), BF16),
            pltpu.VMEM((768, 1024), BF16),
        ],
        compiler_params=grant(16),
    )(received)


def plane_gram_kernel(core_ref, r_ref, g_ref, start_ref, turned_ref, mine_ref, other_ref, wh_ref, wl_ref, red_ref):
    folded = jnp.sum(g_ref[...], axis=0)
    gram = jnp.concatenate([folded[:, 0:64], folded[:, 64:128]], axis=0)
    start = jnp.concatenate([start_ref[...], jnp.zeros((64, 112), F32)], axis=1)
    basis = subspace_narrow(gram, start)[:, 0:16]
    widen = jnp.where(
        lax.broadcasted_iota(jnp.int32, (16, 256), 1) // 16 == lax.broadcasted_iota(jnp.int32, (16, 256), 0), 1.0, 0.0
    ).astype(F32)
    wide = exact_dot(basis, widen)
    keep = (
        lax.broadcasted_iota(jnp.int32, (128, 256), 0) // 8 == lax.broadcasted_iota(jnp.int32, (128, 256), 1) % 16
    )
    for s in range(8):
        weights = jnp.where(keep, jnp.concatenate([wide[8 * s : 8 * s + 8]] * 16, axis=0), 0.0)
        high, low = split2(weights)
        wh_ref[128 * s : 128 * (s + 1), :] = high
        wl_ref[128 * s : 128 * (s + 1), :] = low
    total = None
    for s in range(8):
        high, low = split2(r_ref[s])
        rows = slice(128 * s, 128 * (s + 1))
        term = bf16_dot(high, wh_ref[rows]) + bf16_dot(high, wl_ref[rows]) + bf16_dot(low, wh_ref[rows])
        total = term if s == 0 else total + term
    red_ref[...] = total
    lane = lax.broadcasted_iota(jnp.int32, (16, 128), 1)
    blank = jnp.zeros((8, 256), F32)
    for a in range(8):
        rows = []
        for b in range(4):
            g = 4 * a + b
            rows += [red_ref[24 * g : 24 * g + 24, :], blank]
        turned = jnp.concatenate(rows, axis=0).T
        shifted = [turned] + [pltpu.roll(turned, 32 * k, 1) for k in range(1, 4)]
        for b in range(4):
            g = 4 * a + b
            for quad in range(4):
                block = None
                for k in range(4):
                    r = 4 * quad + k
                    piece = shifted[(k - b) % 4][16 * r : 16 * r + 16, :]
                    block = piece if k == 0 else jnp.where(lane // 32 == k, piece, block)
                turned_ref[16 * g : 16 * g + 16, 128 * quad : 128 * (quad + 1)] = block
    high, low = split2(turned_ref[...])
    left = jnp.concatenate([high, high, low], axis=1)
    right = jnp.concatenate([high, low, high], axis=1)
    blocks = []
    for i in range(4):
        for j in range(i, 4):
            blocks.append(bf16_dot(left[128 * i : 128 * (i + 1)], right[128 * j : 128 * (j + 1)], NT))
    first = core_ref[0] == 0
    for n in range(5):
        rows = slice(128 * n, 128 * (n + 1))
        mine_ref[rows, :] = jnp.where(first, blocks[n], blocks[n + 5])
        other_ref[rows, :] = jnp.where(first, blocks[n + 5], blocks[n])


def plane_gram(core, received, grams, start_species):
    half = jax.ShapeDtypeStruct((640, 128), F32)
    whole = pl.BlockSpec(memory_space=pltpu.VMEM)
    return pl.pallas_call(
        plane_gram_kernel,
        out_shape=(jax.ShapeDtypeStruct((512, 512), F32), half, half),
        in_specs=[pl.BlockSpec(memory_space=pltpu.SMEM), whole, whole, whole],
        scratch_shapes=[pltpu.VMEM((1024, 256), BF16), pltpu.VMEM((1024, 256), BF16), pltpu.VMEM((768, 256), F32)],
        compiler_params=grant(20),
    )(core, received, grams, start_species)


def core_kernel(core_ref, mine_ref, other_ref, turned_ref, start_ref, out_ref, peaks_ref, image_ref):
    first = core_ref[0] == 0
    blocks = {}
    n = 0
    for i in range(4):
        for j in range(i, 4):
            rows = slice(128 * (n % 5), 128 * (n % 5 + 1))
            mine, other = mine_ref[rows, :], other_ref[rows, :]
            blocks[i, j] = jnp.where(first, mine, other) if n < 5 else jnp.where(first, other, mine)
            if i != j:
                blocks[j, i] = blocks[i, j].T
            n += 1
    gram = jnp.concatenate(
        [jnp.concatenate([blocks[i, j] for j in range(4)], axis=1) for i in range(4)], axis=0
    )
    basis = subspace(gram, start_ref[...], image_ref)
    th, tl = split2(turned_ref[...].T)
    bh, bl = split2(basis)
    core = bf16_dot(th, bh) + bf16_dot(th, bl) + bf16_dot(tl, bh)
    for r in range(16):
        out_ref[pl.ds(r, 24, stride=16), :] = core[32 * r : 32 * r + 24, :]
    peaks = jnp.max(jnp.abs(core).reshape(16, 32, 128), axis=2)
    peaks_ref[...] = peaks.T[0:24]


def core_of(core, mine, other, turned, start_plane):
    whole = pl.BlockSpec(memory_space=pltpu.VMEM)
    return pl.pallas_call(
        core_kernel,
        out_shape=(jax.ShapeDtypeStruct((384, 128), F32), jax.ShapeDtypeStruct((24, 16), F32)),
        in_specs=[pl.BlockSpec(memory_space=pltpu.SMEM), whole, whole, whole, whole],
        scratch_shapes=[pltpu.VMEM((512, 128), F32)],
        compiler_params=grant(20),
    )(core, mine, other, turned, start_plane)


def over_plane(x):
    return lax.all_to_all(x, "gx", 0, 0, tiled=True, axis_index_groups=PLANES)


def copies(x, count):
    return jnp.broadcast_to(x[None], (count,) + x.shape)


def per_device(tensor, start_species, start_plane):
    core = (lax.axis_index("gx") % 2).astype(jnp.int32).reshape(1)
    sent = cells_first(tensor).reshape(256, 24, 128)
    received = lax.all_to_all(sent, BOTH, 0, 0, tiled=True).reshape(8, 768, 128)
    grams = species_gram(received)
    grams = grams + lax.ppermute(grams, "gx", PAIR)
    grams = jnp.sum(over_plane(copies(grams, 16)), axis=0)
    grams = lax.all_to_all(copies(grams, 8), "sp", 0, 0, tiled=True)
    turned, mine, other = plane_gram(core, received, grams, start_species)
    mine = mine + lax.ppermute(other, "gx", PAIR)
    share = jnp.sum(over_plane(mine.reshape(16, 40, 128)), axis=0)
    share = jnp.sum(lax.all_to_all(copies(share, 8), "sp", 0, 0, tiled=True), axis=0)
    mine = over_plane(copies(share, 16)).reshape(640, 128)
    other = lax.ppermute(mine, "gx", PAIR)
    core_block, block_peaks = core_of(core, mine, other, turned, start_plane)
    return core_block.reshape(24, 16, 128), block_peaks


def solution(mesh):
    placed = (P("sp", "gx", None), P(), P())
    return jax.shard_map(
        per_device,
        mesh=mesh,
        in_specs=placed,
        out_specs=(P(BOTH, None, None), P(BOTH, None)),
        check_vma=False,
    )
```

```python
import jax
import jax.numpy as jnp
from jax import lax
from jax.experimental import pallas as pl
from jax.experimental.pallas import tpu as pltpu
from jax.sharding import PartitionSpec as P

SWEEPS = 4
HEIGHT = 2
CHUNKS = 4
SPARE = 32768
F32 = jnp.float32
BF16 = jnp.bfloat16
BOTH = ("sp", "gx")
NN = (((1,), (0,)), ((), ()))
NT = (((1,), (1,)), ((), ()))
TN = (((0,), (0,)), ((), ()))
PAIR = [(d, d ^ 1) for d in range(32)]
PLANES = [[d + core for d in range(0, 32, 2)] for core in range(2)]


def grant(mebibytes):
    return pltpu.CompilerParams(vmem_limit_bytes=mebibytes * 1024 * 1024)


def exact_dot(a, b, dims=NN):
    return lax.dot_general(a, b, dims, precision=lax.Precision.HIGHEST, preferred_element_type=F32)


def bf16_dot(a, b, dims=NN):
    return lax.dot_general(a, b, dims, preferred_element_type=F32)


def split2(x):
    high = x.astype(BF16)
    return high, (x - high.astype(F32)).astype(BF16)


def split3(x):
    high = x.astype(BF16)
    rest = x - high.astype(F32)
    mid = rest.astype(BF16)
    return high, mid, (rest - mid.astype(F32)).astype(BF16)


def six(a, b, dims=NN):
    (ah, am, al), (bh, bm, bl) = a, b
    (ka,), (kb,) = dims[0]
    n = bh.shape[1 - kb]
    left = jnp.concatenate([ah, am], axis=ka)
    right = jnp.concatenate([jnp.concatenate([x, x], axis=kb) for x in (bh, bm)], axis=1 - kb)
    main = bf16_dot(left, right, dims)
    rest = bf16_dot(jnp.concatenate([al, ah], axis=ka), jnp.concatenate([bh, bl], axis=kb), dims)
    return main[:, :n] + (main[:, n:] + rest)


def six_gram(a):
    high, mid, low = a
    left = jnp.concatenate([high, mid, low], axis=1)
    got = bf16_dot(left, jnp.concatenate([high, mid], axis=1), TN)
    small = got[256:384, 0:128]
    cross = got[0:128, 128:256] + got[128:256, 0:128]
    return got[0:128, 0:128] + (cross + (got[128:256, 128:256] + (small + small.T)))


def across(x, j):
    return jnp.broadcast_to(x[:, j : j + 1], (8, 128))


def full_row(x, i):
    return jnp.broadcast_to(x[i : i + 1, :], (8, 128))


def inverse_factor(panels, height=1, between=None):
    count = len(panels)
    sub = lax.broadcasted_iota(jnp.int32, (8, 128), 0)
    lane = lax.broadcasted_iota(jnp.int32, (8, 128), 1)
    state = list(panels)
    result = []
    for p in range(0, count, height):
        width = 8 * height
        own = (lane >= 8 * p) & (lane < 8 * p + width)
        cols = [[across(state[p + t], 8 * p + j) for t in range(height)] for j in range(width)]
        solved = [
            jnp.where(own, jnp.where(lane == sub + 8 * (p + t), 1.0, 0.0), state[p + t]) for t in range(height)
        ]
        rows = [jnp.where(lane < 8 * p + width, x, 0.0) for x in solved]
        root = [None] * height
        diag = full_row(cols[0][0], 0)
        for j in range(width):
            tj, ij = divmod(j, 8)
            recip = 1.0 / diag
            pivots = [full_row(cols[k][tj], ij) for k in range(j + 1, width)]
            if j + 1 < width:
                tn, i_n = divmod(j + 1, 8)
                diag = full_row(cols[j + 1][tn], i_n) - (full_row(cols[j][tn], i_n) * pivots[0]) * recip
            root[tj] = recip if ij == 0 else jnp.where(sub == ij, recip, root[tj])
            mult = []
            for t in range(height):
                m = cols[j][t] * recip
                mult.append(jnp.where(sub == ij, 0.0, m) if t == tj else m)
            for k in range(j + 1, width):
                cols[k] = [cols[k][t] - mult[t] * pivots[k - j - 1] for t in range(height)]
            pivot = full_row(solved[tj], ij)
            solved = [solved[t] - mult[t] * pivot for t in range(height)]
            pivot = full_row(rows[tj], ij)
            for t in range(tj, height):
                m = jnp.where(sub > ij, mult[t], 0.0) if t == tj else mult[t]
                rows[t] = rows[t] - m * pivot
        for t in range(height):
            result.append(rows[t] * jnp.sqrt(root[t]))
            solved[t] = solved[t] * root[t]
        near = min(p + 2 * height, count)
        for k in range(p + height, near):
            fresh = jnp.where(own, 0.0, state[k])
            for j in range(width):
                tj, ij = divmod(j, 8)
                fresh = fresh - across(state[k], 8 * p + j) * full_row(solved[tj], ij)
            state[k] = fresh
        if near < count:
            far = jnp.concatenate(state[near:], axis=0)
            ends = [jnp.zeros((8 * n, 128), F32) for n in (p, 16 - p - height)]
            weights = jnp.concatenate(([ends[0]] if p else []) + solved + [ends[1]], axis=0)
            change = six(split3(far), split3(weights))
            for k in range(near, count):
                at = 8 * (k - near)
                state[k] = jnp.where(own, 0.0, state[k]) - change[at : at + 8]
        if between is not None:
            between(p // height)
    return result


def subspace(gram, start, image_ref):
    split_gram = split3(gram)
    image_block = six(split_gram, split3(start))
    chunk = gram.shape[0] // CHUNKS
    for sweep in range(SWEEPS):
        pieces = split3(image_block)
        inner = six_gram(pieces)
        last = sweep + 1 == SWEEPS

        def ahead(panel):
            if panel < CHUNKS and not last:
                rows = slice(chunk * panel, chunk * (panel + 1))
                image_ref[rows, :] = six(tuple(g[rows] for g in split_gram), pieces)

        tiles = [inner[8 * p : 8 * p + 8] for p in range(16)]
        factor = split3(jnp.concatenate(inverse_factor(tiles, HEIGHT, ahead), axis=0))
        image_block = six(pieces if last else split3(image_ref[...]), factor, NT)
    return image_block


def subspace_narrow(gram, start, between):
    split_gram = split3(gram)
    image_block = six(split_gram, split3(start))
    blank = jnp.zeros((112, 128), F32)
    for sweep in range(SWEEPS):
        pieces = split3(image_block)
        inner = six_gram(pieces)
        ahead = pieces if sweep + 1 == SWEEPS else split3(six(split_gram, pieces))
        between(sweep)
        factor = inverse_factor([inner[0:8], inner[8:16]], 2)
        image_block = six(ahead, split3(jnp.concatenate(factor + [blank], axis=0)), NT)
    return image_block


STEPS = 8


def cells_first_kernel(x_ref, o_ref, tile_ref, turned_ref, in_sems, out_sems):
    step = o_ref.shape[0] // STEPS
    loads = [
        pltpu.make_async_copy(x_ref.at[:, pl.ds(step * k, step)], tile_ref.at[k], in_sems.at[k]) for k in range(STEPS)
    ]
    stores = [
        pltpu.make_async_copy(turned_ref.at[k], o_ref.at[pl.ds(step * k, step)], out_sems.at[k]) for k in range(STEPS)
    ]
    for load in loads:
        load.start()
    for k in range(STEPS):
        loads[k].wait()
        for n in range(step // 128):
            tile = tile_ref[k, :, 128 * n : 128 * (n + 1)].reshape(8, 16, 128)
            rows = jnp.concatenate([tile[:, x, :] for x in range(16)], axis=0)
            turned_ref[k, 128 * n : 128 * (n + 1), :] = rows.T
        stores[k].start()
    for store in stores:
        store.wait()


def cells_first(block):
    cells = block.shape[2]
    step = cells // STEPS
    return pl.pallas_call(
        cells_first_kernel,
        out_shape=jax.ShapeDtypeStruct((cells, 128), F32),
        in_specs=[pl.BlockSpec(memory_space=pltpu.HBM)],
        out_specs=pl.BlockSpec(memory_space=pltpu.HBM),
        scratch_shapes=[
            pltpu.VMEM((STEPS, 128, step), F32),
            pltpu.VMEM((STEPS, step, 128), F32),
            pltpu.SemaphoreType.DMA((STEPS,)),
            pltpu.SemaphoreType.DMA((STEPS,)),
        ],
        compiler_params=grant(56),
    )(block.reshape(128, cells))


def species_gram_kernel(r_ref, o_ref, ht_ref, h_ref, l_ref):
    for s in range(8):
        high, low = split2(r_ref[s])
        ht_ref[128 * s : 128 * (s + 1), :] = r_ref[s].T.astype(BF16)
        h_ref[:, 128 * s : 128 * (s + 1)] = high
        l_ref[:, 128 * s : 128 * (s + 1)] = low
    lane = lax.broadcasted_iota(jnp.int32, (8, 256), 1) % 128
    rows = []
    for a in range(4):
        left = ht_ref[256 * a : 256 * (a + 1), :]
        parts = [[], []]
        for b in range(4):
            right = slice(256 * b, 256 * (b + 1))
            prod = bf16_dot(left, l_ref[:, right])
            if b >= a:
                main = bf16_dot(left, h_ref[:, right])
                prod = prod + (main if b > a else 0.5 * main)
            for half in range(2):
                acc = prod[128 * half : 128 * half + 8]
                for x in range(1, 16):
                    acc = jnp.where(lane // 8 == x, prod[128 * half + 8 * x : 128 * half + 8 * x + 8], acc)
                parts[half].append(acc)
        for half in range(2):
            rows.append(jnp.concatenate(parts[half], axis=1))
    wide = jnp.concatenate(rows, axis=0)
    fold = jnp.where(
        lax.broadcasted_iota(jnp.int32, (1024, 64), 0) // 128 * 8
        + lax.broadcasted_iota(jnp.int32, (1024, 64), 0) % 8
        == lax.broadcasted_iota(jnp.int32, (1024, 64), 1),
        1.0,
        0.0,
    ).astype(F32)
    half = exact_dot(wide, fold)
    gram = half + half.T
    o_ref[...] = jnp.concatenate([gram[0:32], gram[32:64]], axis=1)


def species_gram(received):
    return pl.pallas_call(
        species_gram_kernel,
        out_shape=jax.ShapeDtypeStruct((32, 128), F32),
        scratch_shapes=[
            pltpu.VMEM((1024, 768), BF16),
            pltpu.VMEM((768, 1024), BF16),
            pltpu.VMEM((768, 1024), BF16),
        ],
        compiler_params=grant(16),
    )(received)


def plane_gram_kernel(
    core_ref, r_ref, g_ref, start_ref, out_ref, mine_ref, other_ref, wh_ref, wl_ref, h_ref, l_ref, red_ref, turned_ref, sem
):
    def between(sweep):
        for s in (2 * sweep, 2 * sweep + 1):
            lanes = slice(128 * s, 128 * (s + 1))
            h_ref[:, lanes], l_ref[:, lanes] = split2(r_ref[s])

    folded = jnp.sum(g_ref[...], axis=0)
    gram = jnp.concatenate([folded[:, 0:64], folded[:, 64:128]], axis=0)
    start = jnp.concatenate([start_ref[...], jnp.zeros((112, 64), F32)], axis=0).T
    basis = subspace_narrow(gram, start, between)[:, 0:16]
    widen = jnp.where(
        lax.broadcasted_iota(jnp.int32, (16, 256), 1) // 16 == lax.broadcasted_iota(jnp.int32, (16, 256), 0), 1.0, 0.0
    ).astype(BF16)
    high, mid, low = split3(basis)
    wide = bf16_dot(jnp.concatenate([high, mid, low], axis=1), jnp.concatenate([widen] * 3, axis=0))
    keep = (
        lax.broadcasted_iota(jnp.int32, (128, 256), 0) // 8 == lax.broadcasted_iota(jnp.int32, (128, 256), 1) % 16
    )
    for s in range(8):
        weights = jnp.where(keep, jnp.concatenate([wide[8 * s : 8 * s + 8]] * 16, axis=0), 0.0)
        high, low = split2(weights)
        wh_ref[128 * s : 128 * (s + 1), :] = high
        wl_ref[128 * s : 128 * (s + 1), :] = low
    wh = wh_ref[...]
    total = bf16_dot(h_ref[...], wh) + (bf16_dot(h_ref[...], wl_ref[...]) + bf16_dot(l_ref[...], wh))
    red_ref[...] = total
    lane = lax.broadcasted_iota(jnp.int32, (16, 128), 1)
    blank = jnp.zeros((8, 256), F32)
    for a in range(8):
        rows = []
        for b in range(4):
            g = 4 * a + b
            rows += [red_ref[24 * g : 24 * g + 24, :], blank]
        turned = jnp.concatenate(rows, axis=0).T
        shifted = [turned] + [pltpu.roll(turned, 32 * k, 1) for k in range(1, 4)]
        for b in range(4):
            g = 4 * a + b
            for quad in range(4):
                block = None
                for k in range(4):
                    r = 4 * quad + k
                    piece = shifted[(k - b) % 4][16 * r : 16 * r + 16, :]
                    block = piece if k == 0 else jnp.where(lane // 32 == k, piece, block)
                turned_ref[16 * g : 16 * g + 16, 128 * quad : 128 * (quad + 1)] = block
    copy = pltpu.make_async_copy(turned_ref, out_ref.at[pl.ds(0, 512)], sem)
    copy.start()
    high, low = split2(turned_ref[...])
    left = jnp.concatenate([high, high, low], axis=1)
    right = jnp.concatenate([high, low, high], axis=1)
    blocks = []
    for i in range(4):
        for j in range(i, 4):
            blocks.append(bf16_dot(left[128 * i : 128 * (i + 1)], right[128 * j : 128 * (j + 1)], NT))
    first = core_ref[0] == 0
    for n in range(5):
        rows = slice(128 * n, 128 * (n + 1))
        mine_ref[rows, :] = jnp.where(first, blocks[n], blocks[n + 5])
        other_ref[rows, :] = jnp.where(first, blocks[n + 5], blocks[n])
    copy.wait()


def plane_gram(core, received, grams, start_species):
    half = jax.ShapeDtypeStruct((640, 128), F32)
    whole = pl.BlockSpec(memory_space=pltpu.VMEM)
    return pl.pallas_call(
        plane_gram_kernel,
        out_shape=(jax.ShapeDtypeStruct((SPARE, 512), F32), half, half),
        in_specs=[pl.BlockSpec(memory_space=pltpu.SMEM), whole, whole, whole],
        out_specs=(pl.BlockSpec(memory_space=pltpu.HBM), whole, whole),
        scratch_shapes=[
            pltpu.VMEM((1024, 256), BF16),
            pltpu.VMEM((1024, 256), BF16),
            pltpu.VMEM((768, 1024), BF16),
            pltpu.VMEM((768, 1024), BF16),
            pltpu.VMEM((768, 256), F32),
            pltpu.VMEM((512, 512), F32),
            pltpu.SemaphoreType.DMA,
        ],
        compiler_params=grant(20),
    )(core, received, grams, start_species.T)


def core_kernel(
    core_ref, mine_ref, other_ref, turned_hbm, start_ref, out_ref, peaks_ref, image_ref, turned_ref, sem
):
    copy = pltpu.make_async_copy(turned_hbm.at[pl.ds(0, 512)], turned_ref, sem)
    copy.start()
    first = core_ref[0] == 0
    blocks = {}
    n = 0
    for i in range(4):
        for j in range(i, 4):
            rows = slice(128 * (n % 5), 128 * (n % 5 + 1))
            mine, other = mine_ref[rows, :], other_ref[rows, :]
            blocks[i, j] = jnp.where(first, mine, other) if n < 5 else jnp.where(first, other, mine)
            if i != j:
                blocks[j, i] = blocks[i, j].T
            n += 1
    gram = jnp.concatenate(
        [jnp.concatenate([blocks[i, j] for j in range(4)], axis=1) for i in range(4)], axis=0
    )
    basis = subspace(gram, start_ref[...], image_ref)
    copy.wait()
    th, tl = split2(turned_ref[...].T)
    bh, bl = split2(basis)
    core = bf16_dot(th, bh) + bf16_dot(th, bl) + bf16_dot(tl, bh)
    for r in range(16):
        out_ref[pl.ds(r, 24, stride=16), :] = core[32 * r : 32 * r + 24, :]
    peaks = jnp.max(jnp.abs(core).reshape(16, 32, 128), axis=2)
    peaks_ref[...] = peaks[:, 0:24]


def core_of(core, mine, other, turned, start_plane):
    whole = pl.BlockSpec(memory_space=pltpu.VMEM)
    return pl.pallas_call(
        core_kernel,
        out_shape=(jax.ShapeDtypeStruct((384, 128), F32), jax.ShapeDtypeStruct((16, 24), F32)),
        in_specs=[pl.BlockSpec(memory_space=pltpu.SMEM), whole, whole, pl.BlockSpec(memory_space=pltpu.HBM), whole],
        scratch_shapes=[pltpu.VMEM((512, 128), F32), pltpu.VMEM((512, 512), F32), pltpu.SemaphoreType.DMA],
        compiler_params=grant(20),
    )(core, mine, other, turned, start_plane)


def over_plane(x):
    return lax.all_to_all(x, "gx", 0, 0, tiled=True, axis_index_groups=PLANES)


def copies(x, count):
    return jnp.broadcast_to(x[None], (count,) + x.shape)


def per_device(tensor, start_species, start_plane):
    core = (lax.axis_index("gx") % 2).astype(jnp.int32).reshape(1)
    sent = cells_first(tensor).reshape(256, 24, 128)
    received = lax.all_to_all(sent, BOTH, 0, 0, tiled=True).reshape(8, 768, 128)
    grams, core = lax.optimization_barrier((species_gram(received), core))
    grams = grams + lax.ppermute(grams, "gx", PAIR)
    grams = jnp.sum(over_plane(copies(grams, 16)), axis=0)
    grams = lax.all_to_all(copies(grams, 8), "sp", 0, 0, tiled=True)
    turned, mine, other = plane_gram(core, received, grams, start_species)
    mine = mine + lax.ppermute(other, "gx", PAIR)
    share = jnp.sum(over_plane(mine.reshape(16, 40, 128)), axis=0)
    share = jnp.sum(lax.all_to_all(copies(share, 8), "sp", 0, 0, tiled=True), axis=0)
    mine = over_plane(copies(share, 16)).reshape(640, 128)
    other = lax.ppermute(mine, "gx", PAIR)
    core_block, block_peaks = core_of(core, mine, other, turned, start_plane)
    return core_block.reshape(24, 16, 128), block_peaks.T


def solution(mesh):
    placed = (P("sp", "gx", None), P(), P())
    return jax.shard_map(
        per_device,
        mesh=mesh,
        in_specs=placed,
        out_specs=(P(BOTH, None, None), P(BOTH, None)),
        check_vma=False,
    )
```

```python
import jax
import jax.numpy as jnp
from jax import lax
from jax.experimental import pallas as pl
from jax.experimental.pallas import tpu as pltpu
from jax.sharding import PartitionSpec as P

SWEEPS = 4
CHUNKS = 4
SPARE = 32768
F32 = jnp.float32
BF16 = jnp.bfloat16
BOTH = ("sp", "gx")
NN = (((1,), (0,)), ((), ()))
NT = (((1,), (1,)), ((), ()))
TN = (((0,), (0,)), ((), ()))
PAIR = [(d, d ^ 1) for d in range(32)]
PLANES = [[d + core for d in range(0, 32, 2)] for core in range(2)]


def grant(mebibytes):
    return pltpu.CompilerParams(vmem_limit_bytes=mebibytes * 1024 * 1024)


def exact_dot(a, b, dims=NN):
    return lax.dot_general(a, b, dims, precision=lax.Precision.HIGHEST, preferred_element_type=F32)


def bf16_dot(a, b, dims=NN):
    return lax.dot_general(a, b, dims, preferred_element_type=F32)


def split2(x):
    high = x.astype(BF16)
    return high, (x - high.astype(F32)).astype(BF16)


def split3(x):
    high = x.astype(BF16)
    rest = x - high.astype(F32)
    mid = rest.astype(BF16)
    return high, mid, (rest - mid.astype(F32)).astype(BF16)


def six(a, b, dims=NN):
    (ah, am, al), (bh, bm, bl) = a, b
    (ka,), (kb,) = dims[0]
    n = bh.shape[1 - kb]
    left = jnp.concatenate([ah, am], axis=ka)
    right = jnp.concatenate([jnp.concatenate([x, x], axis=kb) for x in (bh, bm)], axis=1 - kb)
    main = bf16_dot(left, right, dims)
    rest = bf16_dot(jnp.concatenate([al, ah], axis=ka), jnp.concatenate([bh, bl], axis=kb), dims)
    return main[:, :n] + (main[:, n:] + rest)


def six_gram(a):
    high, mid, low = a
    left = jnp.concatenate([high, mid, low], axis=1)
    got = bf16_dot(left, jnp.concatenate([high, mid], axis=1), TN)
    small = got[256:384, 0:128]
    cross = got[0:128, 128:256] + got[128:256, 0:128]
    return got[0:128, 0:128] + (cross + (got[128:256, 128:256] + (small + small.T)))


def across(x, j):
    return jnp.broadcast_to(x[:, j : j + 1], (8, 128))


def full_row(x, i):
    return jnp.broadcast_to(x[i : i + 1, :], (8, 128))


def inverse_factor(tiles, between=None):
    count = len(tiles)
    sub = lax.broadcasted_iota(jnp.int32, (8, 128), 0)
    lane = lax.broadcasted_iota(jnp.int32, (8, 128), 1)
    state = list(tiles)
    result = []
    for p in range(0, count, 2):
        at = 8 * p
        own_a, own_b = (lane >= at) & (lane < at + 8), (lane >= at + 8) & (lane < at + 16)
        unit_a = jnp.where(lane == sub + at, 1.0, 0.0)
        unit_b = jnp.where(lane == sub + at + 8, 1.0, 0.0)
        cols = [across(state[p], at + j) for j in range(8)]
        below = [across(state[p + 1], at + j) for j in range(8)]
        right = [across(state[p + 1], at + 8 + j) for j in range(8)]
        top = jnp.where(own_a, unit_a, state[p])
        low = jnp.where(own_a, 0.0, state[p + 1])
        diag = full_row(cols[0], 0)
        for j in range(8):
            recip = 1.0 / diag
            pivots = [full_row(cols[k], j) for k in range(j + 1, 8)]
            crossing = [full_row(below[j], k) for k in range(8)]
            if j < 7:
                diag = full_row(cols[j + 1], j + 1) - (full_row(cols[j], j + 1) * pivots[0]) * recip
            else:
                diag = full_row(right[0], 0) - (crossing[0] * crossing[0]) * recip
            root_a = recip if j == 0 else jnp.where(sub == j, recip, root_a)
            up = jnp.where(sub == j, 0.0, cols[j] * recip)
            down = below[j] * recip
            for k in range(j + 1, 8):
                cols[k] = cols[k] - up * pivots[k - j - 1]
                below[k] = below[k] - down * pivots[k - j - 1]
            for k in range(8):
                right[k] = right[k] - down * crossing[k]
            forward_a = top if j == 0 else jnp.where(sub == j, top, forward_a)
            pivot = full_row(top, j)
            top, low = top - up * pivot, low - down * pivot
        top = top * root_a
        mixed = [across(top, at + 8 + k) for k in range(8)]
        top = jnp.where(own_b, 0.0, top)
        low = jnp.where(own_b, unit_b, low)
        for j in range(8):
            recip = 1.0 / diag
            pivots = [full_row(right[k], j) for k in range(j + 1, 8)]
            if j < 7:
                diag = full_row(right[j + 1], j + 1) - (full_row(right[j], j + 1) * pivots[0]) * recip
            root_b = recip if j == 0 else jnp.where(sub == j, recip, root_b)
            up = jnp.where(sub == j, 0.0, right[j] * recip)
            for k in range(j + 1, 8):
                right[k] = right[k] - up * pivots[k - j - 1]
            forward_b = low if j == 0 else jnp.where(sub == j, low, forward_b)
            low = low - up * full_row(low, j)
        low = low * root_b
        result.append(jnp.where(lane < at + 8, forward_a * jnp.sqrt(root_a), 0.0))
        result.append(jnp.where(lane < at + 16, forward_b * jnp.sqrt(root_b), 0.0))
        low_rows = [full_row(low, k) for k in range(8)]
        for k in range(8):
            top = top - mixed[k] * low_rows[k]
        own = own_a | own_b
        near = min(p + 4, count)
        for k in range(p + 2, near):
            one = jnp.where(own, 0.0, state[k])
            for j in range(8):
                one = one - across(state[k], at + 8 + j) * low_rows[j]
            two = across(state[k], at) * full_row(top, 0)
            for j in range(1, 8):
                two = two + across(state[k], at + j) * full_row(top, j)
            state[k] = one - two
        if near < count:
            far = jnp.concatenate(state[near:], axis=0)
            ends = [jnp.zeros((8 * n, 128), F32) for n in (p, 14 - p)]
            weights = jnp.concatenate(([ends[0]] if p else []) + [top, low, ends[1]], axis=0)
            change = six(split3(far), split3(weights))
            for k in range(near, count):
                rows = slice(8 * (k - near), 8 * (k - near) + 8)
                state[k] = jnp.where(own, 0.0, state[k]) - change[rows]
        if between is not None:
            between(p // 2)
    return result


def subspace(gram, start, image_ref):
    split_gram = split3(gram)
    image_block = six(split_gram, split3(start))
    chunk = gram.shape[0] // CHUNKS
    for sweep in range(SWEEPS):
        pieces = split3(image_block)
        inner = six_gram(pieces)
        last = sweep + 1 == SWEEPS

        def ahead(panel):
            if panel < CHUNKS and not last:
                rows = slice(chunk * panel, chunk * (panel + 1))
                image_ref[rows, :] = six(tuple(g[rows] for g in split_gram), pieces)

        tiles = [inner[8 * p : 8 * p + 8] for p in range(16)]
        factor = split3(jnp.concatenate(inverse_factor(tiles, ahead), axis=0))
        image_block = six(pieces if last else split3(image_ref[...]), factor, NT)
    return image_block


def subspace_narrow(gram, start, between):
    split_gram = split3(gram)
    image_block = six(split_gram, split3(start))
    blank = jnp.zeros((112, 128), F32)
    for sweep in range(SWEEPS):
        pieces = split3(image_block)
        inner = six_gram(pieces)
        ahead = pieces if sweep + 1 == SWEEPS else split3(six(split_gram, pieces))
        between(sweep)
        factor = inverse_factor([inner[0:8], inner[8:16]])
        image_block = six(ahead, split3(jnp.concatenate(factor + [blank], axis=0)), NT)
    return image_block


STEPS = 8


def cells_first_kernel(x_ref, o_ref, tile_ref, sems):
    step = o_ref.shape[0] // STEPS
    loads = [pltpu.make_async_copy(x_ref.at[:, pl.ds(step * k, step)], tile_ref.at[k], sems.at[k]) for k in range(STEPS)]
    for load in loads:
        load.start()
    for k in range(STEPS):
        loads[k].wait()
        for n in range(step // 128):
            tile = tile_ref[k, :, 128 * n : 128 * (n + 1)].reshape(8, 16, 128)
            rows = jnp.concatenate([tile[:, x, :] for x in range(16)], axis=0)
            at = step * k + 128 * n
            o_ref[at : at + 128, :] = rows.T


def cells_first(block):
    cells = block.shape[2]
    step = cells // STEPS
    return pl.pallas_call(
        cells_first_kernel,
        out_shape=jax.ShapeDtypeStruct((cells, 128), F32),
        in_specs=[pl.BlockSpec(memory_space=pltpu.HBM)],
        out_specs=pl.BlockSpec(memory_space=pltpu.VMEM),
        scratch_shapes=[pltpu.VMEM((STEPS, 128, step), F32), pltpu.SemaphoreType.DMA((STEPS,))],
        compiler_params=grant(50),
    )(block.reshape(128, cells))


def species_gram_kernel(r_ref, o_ref, ht_ref, h_ref, l_ref):
    for s in range(8):
        high, low = split2(r_ref[s])
        ht_ref[128 * s : 128 * (s + 1), :] = high.T
        h_ref[:, 128 * s : 128 * (s + 1)] = high
        l_ref[:, 128 * s : 128 * (s + 1)] = low
    lane = lax.broadcasted_iota(jnp.int32, (8, 256), 1) % 128
    rows = []
    for a in range(4):
        left = ht_ref[256 * a : 256 * (a + 1), :]
        parts = [[], []]
        for b in range(4):
            right = slice(256 * b, 256 * (b + 1))
            prod = bf16_dot(left, l_ref[:, right])
            if b >= a:
                main = bf16_dot(left, h_ref[:, right])
                prod = prod + (main if b > a else 0.5 * main)
            for half in range(2):
                acc = prod[128 * half : 128 * half + 8]
                for x in range(1, 16):
                    acc = jnp.where(lane // 8 == x, prod[128 * half + 8 * x : 128 * half + 8 * x + 8], acc)
                parts[half].append(acc)
        for half in range(2):
            rows.append(jnp.concatenate(parts[half], axis=1))
    wide = jnp.concatenate(rows, axis=0)
    fold = jnp.where(
        lax.broadcasted_iota(jnp.int32, (1024, 64), 0) // 128 * 8
        + lax.broadcasted_iota(jnp.int32, (1024, 64), 0) % 8
        == lax.broadcasted_iota(jnp.int32, (1024, 64), 1),
        1.0,
        0.0,
    ).astype(F32)
    half = exact_dot(wide, fold)
    gram = half + half.T
    o_ref[...] = jnp.concatenate([gram[0:32], gram[32:64]], axis=1)


def species_gram(received):
    return pl.pallas_call(
        species_gram_kernel,
        out_shape=jax.ShapeDtypeStruct((32, 128), F32),
        scratch_shapes=[
            pltpu.VMEM((1024, 768), BF16),
            pltpu.VMEM((768, 1024), BF16),
            pltpu.VMEM((768, 1024), BF16),
        ],
        compiler_params=grant(16),
    )(received)


def plane_gram_kernel(
    r_ref, g_ref, start_ref, out_ref, mine_ref, other_ref, wh_ref, wl_ref, h_ref, l_ref, red_ref, turned_ref, sem
):
    def between(sweep):
        for s in (2 * sweep, 2 * sweep + 1):
            lanes = slice(128 * s, 128 * (s + 1))
            h_ref[:, lanes], l_ref[:, lanes] = split2(r_ref[s])

    folded = jnp.sum(g_ref[...], axis=0)
    gram = jnp.concatenate([folded[:, 0:64], folded[:, 64:128]], axis=0)
    start = jnp.concatenate([start_ref[...], jnp.zeros((112, 64), F32)], axis=0).T
    basis = subspace_narrow(gram, start, between)[:, 0:16]
    column = lax.broadcasted_iota(jnp.int32, (16, 256), 1)
    widen = jnp.where(
        column // 16 % 4 * 4 + column // 64 == lax.broadcasted_iota(jnp.int32, (16, 256), 0), 1.0, 0.0
    ).astype(BF16)
    high, mid, low = split3(basis)
    wide = bf16_dot(jnp.concatenate([high, mid, low], axis=1), jnp.concatenate([widen] * 3, axis=0))
    keep = (
        lax.broadcasted_iota(jnp.int32, (128, 256), 0) // 8 == lax.broadcasted_iota(jnp.int32, (128, 256), 1) % 16
    )
    for s in range(8):
        weights = jnp.where(keep, jnp.concatenate([wide[8 * s : 8 * s + 8]] * 16, axis=0), 0.0)
        high, low = split2(weights)
        wh_ref[128 * s : 128 * (s + 1), :] = high
        wl_ref[128 * s : 128 * (s + 1), :] = low
    wh = wh_ref[...]
    total = bf16_dot(h_ref[...], wh) + (bf16_dot(h_ref[...], wl_ref[...]) + bf16_dot(l_ref[...], wh))
    red_ref[...] = total
    lane = lax.broadcasted_iota(jnp.int32, (24, 128), 1)
    blank = jnp.zeros((8, 128), F32)
    for pair in range(16):
        rows = []
        for k in range(4):
            lanes = slice(128 * (k // 2), 128 * (k // 2 + 1))
            at = 48 * pair
            first, second = red_ref[at : at + 24, lanes], red_ref[at + 24 : at + 48, lanes]
            if k % 2:
                first = pltpu.roll(first, 64, 1)
            else:
                second = pltpu.roll(second, 64, 1)
            rows += [jnp.where(lane < 64, first, second), blank]
        turned = jnp.concatenate(rows, axis=0).T
        for g in range(2):
            for q in range(4):
                at, to = 64 * g + 16 * q, 32 * pair + 16 * g
                turned_ref[to : to + 16, 128 * q : 128 * (q + 1)] = turned[at : at + 16]
    copy = pltpu.make_async_copy(turned_ref, out_ref.at[pl.ds(0, 512)], sem)
    copy.start()
    high, low = split2(turned_ref[...])
    left = jnp.concatenate([high, high, low], axis=1)
    right = jnp.concatenate([high, low, high], axis=1)
    quarter = [slice(0, 256), slice(256, 512)]
    whole = {
        (i, j): bf16_dot(left[quarter[i]], right[quarter[j]], NT) for i, j in ((0, 0), (0, 1), (1, 1))
    }
    blocks = []
    for i in range(4):
        for j in range(i, 4):
            rows, lanes = slice(128 * (i % 2), 128 * (i % 2 + 1)), slice(128 * (j % 2), 128 * (j % 2 + 1))
            blocks.append(whole[i // 2, j // 2][rows, lanes])
    first = lax.axis_index("gx") % 2 == 0
    for n in range(5):
        rows = slice(128 * n, 128 * (n + 1))
        mine_ref[rows, :] = jnp.where(first, blocks[n], blocks[n + 5])
        other_ref[rows, :] = jnp.where(first, blocks[n + 5], blocks[n])
    copy.wait()


def plane_gram(received, grams, start_species):
    half = jax.ShapeDtypeStruct((640, 128), F32)
    whole = pl.BlockSpec(memory_space=pltpu.VMEM)
    return pl.pallas_call(
        plane_gram_kernel,
        out_shape=(jax.ShapeDtypeStruct((SPARE, 512), F32), half, half),
        in_specs=[whole, whole, whole],
        out_specs=(pl.BlockSpec(memory_space=pltpu.HBM), whole, whole),
        scratch_shapes=[
            pltpu.VMEM((1024, 256), BF16),
            pltpu.VMEM((1024, 256), BF16),
            pltpu.VMEM((768, 1024), BF16),
            pltpu.VMEM((768, 1024), BF16),
            pltpu.VMEM((768, 256), F32),
            pltpu.VMEM((512, 512), F32),
            pltpu.SemaphoreType.DMA,
        ],
        compiler_params=grant(20),
    )(received, grams, start_species.T)


def core_kernel(
    mine_ref, other_ref, turned_hbm, start_ref, out_ref, peaks_ref, image_ref, turned_ref, sem
):
    copy = pltpu.make_async_copy(turned_hbm.at[pl.ds(0, 512)], turned_ref, sem)
    copy.start()
    first = lax.axis_index("gx") % 2 == 0
    blocks = {}
    n = 0
    for i in range(4):
        for j in range(i, 4):
            rows = slice(128 * (n % 5), 128 * (n % 5 + 1))
            mine, other = mine_ref[rows, :], other_ref[rows, :]
            blocks[i, j] = jnp.where(first, mine, other) if n < 5 else jnp.where(first, other, mine)
            if i != j:
                blocks[j, i] = blocks[i, j].T
            n += 1
    gram = jnp.concatenate(
        [jnp.concatenate([blocks[i, j] for j in range(4)], axis=1) for i in range(4)], axis=0
    )
    basis = subspace(gram, start_ref[...], image_ref)
    copy.wait()
    th, tl = split2(turned_ref[...].T)
    bh, bl = split2(basis)
    core = bf16_dot(th, bh) + bf16_dot(th, bl) + bf16_dot(tl, bh)
    for r in range(16):
        out_ref[pl.ds(r, 24, stride=16), :] = core[32 * r : 32 * r + 24, :]
    peaks = jnp.max(jnp.abs(core).reshape(16, 32, 128), axis=2)
    peaks_ref[...] = peaks[:, 0:24]


def core_of(mine, other, turned, start_plane):
    whole = pl.BlockSpec(memory_space=pltpu.VMEM)
    return pl.pallas_call(
        core_kernel,
        out_shape=(jax.ShapeDtypeStruct((384, 128), F32), jax.ShapeDtypeStruct((16, 24), F32)),
        in_specs=[whole, whole, pl.BlockSpec(memory_space=pltpu.HBM), whole],
        scratch_shapes=[pltpu.VMEM((512, 128), F32), pltpu.VMEM((512, 512), F32), pltpu.SemaphoreType.DMA],
        compiler_params=grant(20),
    )(mine, other, turned, start_plane)


def over_plane(x):
    return lax.all_to_all(x, "gx", 0, 0, tiled=True, axis_index_groups=PLANES)


def copies(x, count):
    return jnp.broadcast_to(x[None], (count,) + x.shape)


def per_device(tensor, start_species, start_plane):
    sent = cells_first(tensor).reshape(256, 24, 128)
    received = lax.all_to_all(sent, BOTH, 0, 0, tiled=True).reshape(8, 768, 128)
    grams = species_gram(received)
    grams = grams + lax.ppermute(grams, "gx", PAIR)
    grams = jnp.sum(over_plane(copies(grams, 16)), axis=0)
    grams = lax.all_to_all(copies(grams, 8), "sp", 0, 0, tiled=True)
    turned, mine, other = plane_gram(received, grams, start_species)
    mine = mine + lax.ppermute(other, "gx", PAIR)
    share = jnp.sum(over_plane(mine.reshape(16, 40, 128)), axis=0)
    share = jnp.sum(lax.all_to_all(copies(share, 8), "sp", 0, 0, tiled=True), axis=0)
    mine = over_plane(copies(share, 16)).reshape(640, 128)
    other = lax.ppermute(mine, "gx", PAIR)
    core_block, block_peaks = core_of(mine, other, turned, start_plane)
    return core_block.reshape(24, 16, 128), block_peaks.T


def solution(mesh):
    placed = (P("sp", "gx", None), P(), P())
    return jax.shard_map(
        per_device,
        mesh=mesh,
        in_specs=placed,
        out_specs=(P(BOTH, None, None), P(BOTH, None)),
        check_vma=False,
    )
```

```python
import jax
import jax.numpy as jnp
from jax import lax
from jax.experimental import pallas as pl
from jax.experimental.pallas import tpu as pltpu
from jax.sharding import PartitionSpec as P

SWEEPS = 4
CHUNKS = 4
SPARE = 32768
F32 = jnp.float32
BF16 = jnp.bfloat16
BOTH = ("sp", "gx")
NN = (((1,), (0,)), ((), ()))
NT = (((1,), (1,)), ((), ()))
TN = (((0,), (0,)), ((), ()))
PAIR = [(d, d ^ 1) for d in range(32)]
PLANES = [[d + core for d in range(0, 32, 2)] for core in range(2)]


def grant(mebibytes):
    return pltpu.CompilerParams(vmem_limit_bytes=mebibytes * 1024 * 1024)


def exact_dot(a, b, dims=NN):
    return lax.dot_general(a, b, dims, precision=lax.Precision.HIGHEST, preferred_element_type=F32)


def bf16_dot(a, b, dims=NN):
    return lax.dot_general(a, b, dims, preferred_element_type=F32)


def split2(x):
    high = x.astype(BF16)
    return high, (x - high.astype(F32)).astype(BF16)


def split3(x):
    high = x.astype(BF16)
    rest = x - high.astype(F32)
    mid = rest.astype(BF16)
    return high, mid, (rest - mid.astype(F32)).astype(BF16)


def six(a, b, dims=NN):
    (ah, am, al), (bh, bm, bl) = a, b
    (ka,), (kb,) = dims[0]
    n = bh.shape[1 - kb]
    left = jnp.concatenate([ah, am], axis=ka)
    right = jnp.concatenate([jnp.concatenate([x, x], axis=kb) for x in (bh, bm)], axis=1 - kb)
    main = bf16_dot(left, right, dims)
    rest = bf16_dot(jnp.concatenate([al, ah], axis=ka), jnp.concatenate([bh, bl], axis=kb), dims)
    return main[:, :n] + (main[:, n:] + rest)


def six_gram(a):
    high, mid, low = a
    left = jnp.concatenate([high, mid, low], axis=1)
    got = bf16_dot(left, jnp.concatenate([high, mid], axis=1), TN)
    small = got[256:384, 0:128]
    cross = got[0:128, 128:256] + got[128:256, 0:128]
    return got[0:128, 0:128] + (cross + (got[128:256, 128:256] + (small + small.T)))


def across(x, j):
    return jnp.broadcast_to(x[:, j : j + 1], (8, 128))


def full_row(x, i):
    return jnp.broadcast_to(x[i : i + 1, :], (8, 128))


def inverse_factor(tiles, between=None):
    count = len(tiles)
    sub = lax.broadcasted_iota(jnp.int32, (8, 128), 0)
    lane = lax.broadcasted_iota(jnp.int32, (8, 128), 1)
    state = list(tiles)
    result = []
    for p in range(0, count, 2):
        at = 8 * p
        own_a, own_b = (lane >= at) & (lane < at + 8), (lane >= at + 8) & (lane < at + 16)
        unit_a = jnp.where(lane == sub + at, 1.0, 0.0)
        unit_b = jnp.where(lane == sub + at + 8, 1.0, 0.0)
        cols = [across(state[p], at + j) for j in range(8)]
        below = [across(state[p + 1], at + j) for j in range(8)]
        right = [across(state[p + 1], at + 8 + j) for j in range(8)]
        top = jnp.where(own_a, unit_a, state[p])
        low = jnp.where(own_a, 0.0, state[p + 1])
        diag = full_row(cols[0], 0)
        for j in range(8):
            recip = 1.0 / diag
            pivots = [full_row(cols[k], j) for k in range(j + 1, 8)]
            crossing = [full_row(below[j], k) for k in range(8)]
            if j < 7:
                diag = full_row(cols[j + 1], j + 1) - (full_row(cols[j], j + 1) * pivots[0]) * recip
            else:
                diag = full_row(right[0], 0) - (crossing[0] * crossing[0]) * recip
            root_a = recip if j == 0 else jnp.where(sub == j, recip, root_a)
            up = jnp.where(sub == j, 0.0, cols[j] * recip)
            down = below[j] * recip
            for k in range(j + 1, 8):
                cols[k] = cols[k] - up * pivots[k - j - 1]
                below[k] = below[k] - down * pivots[k - j - 1]
            for k in range(8):
                right[k] = right[k] - down * crossing[k]
            forward_a = top if j == 0 else jnp.where(sub == j, top, forward_a)
            pivot = full_row(top, j)
            top, low = top - up * pivot, low - down * pivot
        top = top * root_a
        mixed = [across(top, at + 8 + k) for k in range(8)]
        top = jnp.where(own_b, 0.0, top)
        low = jnp.where(own_b, unit_b, low)
        for j in range(8):
            recip = 1.0 / diag
            pivots = [full_row(right[k], j) for k in range(j + 1, 8)]
            if j < 7:
                diag = full_row(right[j + 1], j + 1) - (full_row(right[j], j + 1) * pivots[0]) * recip
            root_b = recip if j == 0 else jnp.where(sub == j, recip, root_b)
            up = jnp.where(sub == j, 0.0, right[j] * recip)
            for k in range(j + 1, 8):
                right[k] = right[k] - up * pivots[k - j - 1]
            forward_b = low if j == 0 else jnp.where(sub == j, low, forward_b)
            low = low - up * full_row(low, j)
        low = low * root_b
        result.append(jnp.where(lane < at + 8, forward_a * jnp.sqrt(root_a), 0.0))
        result.append(jnp.where(lane < at + 16, forward_b * jnp.sqrt(root_b), 0.0))
        low_rows = [full_row(low, k) for k in range(8)]
        for k in range(8):
            top = top - mixed[k] * low_rows[k]
        own = own_a | own_b
        near = min(p + 4, count)
        for k in range(p + 2, near):
            one = jnp.where(own, 0.0, state[k])
            for j in range(8):
                one = one - across(state[k], at + 8 + j) * low_rows[j]
            two = across(state[k], at) * full_row(top, 0)
            for j in range(1, 8):
                two = two + across(state[k], at + j) * full_row(top, j)
            state[k] = one - two
        if near < count:
            far = jnp.concatenate(state[near:], axis=0)
            ends = [jnp.zeros((8 * n, 128), F32) for n in (p, 14 - p)]
            weights = jnp.concatenate(([ends[0]] if p else []) + [top, low, ends[1]], axis=0)
            change = six(split3(far), split3(weights))
            for k in range(near, count):
                rows = slice(8 * (k - near), 8 * (k - near) + 8)
                state[k] = jnp.where(own, 0.0, state[k]) - change[rows]
        if between is not None:
            between(p // 2)
    return result


def subspace(gram, start, image_ref):
    split_gram = split3(gram)
    image_block = six(split_gram, split3(start))
    chunk = gram.shape[0] // CHUNKS
    for sweep in range(SWEEPS):
        pieces = split3(image_block)
        inner = six_gram(pieces)
        last = sweep + 1 == SWEEPS

        def ahead(panel):
            if panel < CHUNKS and not last:
                rows = slice(chunk * panel, chunk * (panel + 1))
                image_ref[rows, :] = six(tuple(g[rows] for g in split_gram), pieces)

        tiles = [inner[8 * p : 8 * p + 8] for p in range(16)]
        factor = split3(jnp.concatenate(inverse_factor(tiles, ahead), axis=0))
        image_block = six(pieces if last else split3(image_ref[...]), factor, NT)
    return image_block


def subspace_narrow(gram, start, between):
    split_gram = split3(gram)
    image_block = six(split_gram, split3(start))
    blank = jnp.zeros((112, 128), F32)
    for sweep in range(SWEEPS):
        pieces = split3(image_block)
        inner = six_gram(pieces)
        ahead = pieces if sweep + 1 == SWEEPS else split3(six(split_gram, pieces))
        between(sweep)
        factor = inverse_factor([inner[0:8], inner[8:16]])
        image_block = six(ahead, split3(jnp.concatenate(factor + [blank], axis=0)), NT)
    return image_block


STEPS = 8


def cells_first_kernel(x_ref, o_ref, tile_ref, sems):
    step = o_ref.shape[0] // STEPS
    loads = [pltpu.make_async_copy(x_ref.at[:, pl.ds(step * k, step)], tile_ref.at[k], sems.at[k]) for k in range(STEPS)]
    for load in loads:
        load.start()
    for k in range(STEPS):
        loads[k].wait()
        for n in range(step // 128):
            tile = tile_ref[k, :, 128 * n : 128 * (n + 1)].reshape(8, 16, 128)
            rows = jnp.concatenate([tile[:, x, :] for x in range(16)], axis=0)
            at = step * k + 128 * n
            o_ref[at : at + 128, :] = rows.T


def cells_first(block):
    cells = block.shape[2]
    step = cells // STEPS
    return pl.pallas_call(
        cells_first_kernel,
        out_shape=jax.ShapeDtypeStruct((cells, 128), F32),
        in_specs=[pl.BlockSpec(memory_space=pltpu.HBM)],
        out_specs=pl.BlockSpec(memory_space=pltpu.VMEM),
        scratch_shapes=[pltpu.VMEM((STEPS, 128, step), F32), pltpu.SemaphoreType.DMA((STEPS,))],
        compiler_params=grant(50),
    )(block.reshape(128, cells))


def species_gram_kernel(r_ref, o_ref, ht_ref, h_ref, l_ref):
    for s in range(8):
        high, low = split2(r_ref[s])
        ht_ref[128 * s : 128 * (s + 1), :] = high.T
        h_ref[:, 128 * s : 128 * (s + 1)] = high
        l_ref[:, 128 * s : 128 * (s + 1)] = low
    lane = lax.broadcasted_iota(jnp.int32, (8, 256), 1) % 128
    rows = []
    for a in range(4):
        left = ht_ref[256 * a : 256 * (a + 1), :]
        parts = [[], []]
        for b in range(4):
            right = slice(256 * b, 256 * (b + 1))
            prod = bf16_dot(left, l_ref[:, right])
            if b >= a:
                main = bf16_dot(left, h_ref[:, right])
                prod = prod + (main if b > a else 0.5 * main)
            for half in range(2):
                acc = prod[128 * half : 128 * half + 8]
                for x in range(1, 16):
                    acc = jnp.where(lane // 8 == x, prod[128 * half + 8 * x : 128 * half + 8 * x + 8], acc)
                parts[half].append(acc)
        for half in range(2):
            rows.append(jnp.concatenate(parts[half], axis=1))
    wide = jnp.concatenate(rows, axis=0)
    fold = jnp.where(
        lax.broadcasted_iota(jnp.int32, (1024, 64), 0) // 128 * 8
        + lax.broadcasted_iota(jnp.int32, (1024, 64), 0) % 8
        == lax.broadcasted_iota(jnp.int32, (1024, 64), 1),
        1.0,
        0.0,
    ).astype(F32)
    half = exact_dot(wide, fold)
    gram = half + half.T
    second = jnp.concatenate([gram[48:64, 48:64], gram[16:32, 16:64]], axis=1)
    rows = jnp.concatenate([gram[0:16], second, gram[32:48]], axis=0)
    o_ref[...] = jnp.concatenate([rows[0:24], rows[24:48]], axis=1)


def species_gram(received):
    return pl.pallas_call(
        species_gram_kernel,
        out_shape=jax.ShapeDtypeStruct((24, 128), F32),
        scratch_shapes=[
            pltpu.VMEM((1024, 768), BF16),
            pltpu.VMEM((768, 1024), BF16),
            pltpu.VMEM((768, 1024), BF16),
        ],
        compiler_params=grant(16),
    )(received)


def plane_gram_kernel(
    r_ref, g_ref, start_ref, out_ref, mine_ref, other_ref, wh_ref, wl_ref, h_ref, l_ref, red_ref, turned_ref, sem
):
    def between(sweep):
        for s in (2 * sweep, 2 * sweep + 1):
            lanes = slice(128 * s, 128 * (s + 1))
            h_ref[:, lanes], l_ref[:, lanes] = split2(r_ref[s])

    folded = jnp.sum(g_ref[...], axis=0)
    rows = jnp.concatenate([folded[:, 0:64], folded[:, 64:128]], axis=0)
    across_rows = jnp.concatenate(
        [jnp.concatenate([rows, jnp.zeros((80, 64), F32)], axis=0), jnp.zeros((128, 64), F32)], axis=1
    ).T
    second = jnp.concatenate([across_rows[16:32, 0:16], rows[16:32, 16:64]], axis=1)
    last = jnp.concatenate([across_rows[48:64, 0:48], rows[16:32, 0:16]], axis=1)
    gram = jnp.concatenate([rows[0:16], second, rows[32:48], last], axis=0)
    start = jnp.concatenate([start_ref[...], jnp.zeros((112, 64), F32)], axis=0).T
    basis = subspace_narrow(gram, start, between)[:, 0:16]
    column = lax.broadcasted_iota(jnp.int32, (16, 256), 1)
    widen = jnp.where(
        column // 16 % 4 * 4 + column // 64 == lax.broadcasted_iota(jnp.int32, (16, 256), 0), 1.0, 0.0
    ).astype(BF16)
    high, mid, low = split3(basis)
    wide = bf16_dot(jnp.concatenate([high, mid, low], axis=1), jnp.concatenate([widen] * 3, axis=0))
    keep = (
        lax.broadcasted_iota(jnp.int32, (128, 256), 0) // 8 == lax.broadcasted_iota(jnp.int32, (128, 256), 1) % 16
    )
    for s in range(8):
        weights = jnp.where(keep, jnp.concatenate([wide[8 * s : 8 * s + 8]] * 16, axis=0), 0.0)
        high, low = split2(weights)
        wh_ref[128 * s : 128 * (s + 1), :] = high
        wl_ref[128 * s : 128 * (s + 1), :] = low
    wh = wh_ref[...]
    total = bf16_dot(h_ref[...], wh) + (bf16_dot(h_ref[...], wl_ref[...]) + bf16_dot(l_ref[...], wh))
    red_ref[...] = total
    lane = lax.broadcasted_iota(jnp.int32, (24, 128), 1)
    blank = jnp.zeros((8, 128), F32)
    for pair in range(16):
        rows = []
        for k in range(4):
            lanes = slice(128 * (k // 2), 128 * (k // 2 + 1))
            at = 48 * pair
            first, second = red_ref[at : at + 24, lanes], red_ref[at + 24 : at + 48, lanes]
            if k % 2:
                first = pltpu.roll(first, 64, 1)
            else:
                second = pltpu.roll(second, 64, 1)
            rows += [jnp.where(lane < 64, first, second), blank]
        turned = jnp.concatenate(rows, axis=0).T
        for g in range(2):
            for q in range(4):
                at, to = 64 * g + 16 * q, 32 * pair + 16 * g
                turned_ref[to : to + 16, 128 * q : 128 * (q + 1)] = turned[at : at + 16]
    copy = pltpu.make_async_copy(turned_ref, out_ref.at[pl.ds(0, 512)], sem)
    copy.start()
    high, low = split2(turned_ref[...])
    left = jnp.concatenate([high, high, low], axis=1)
    right = jnp.concatenate([high, low, high], axis=1)
    quarter = [slice(0, 256), slice(256, 512)]
    whole = {
        (i, j): bf16_dot(left[quarter[i]], right[quarter[j]], NT) for i, j in ((0, 0), (0, 1), (1, 1))
    }
    blocks = []
    for i in range(4):
        for j in range(i, 4):
            rows, lanes = slice(128 * (i % 2), 128 * (i % 2 + 1)), slice(128 * (j % 2), 128 * (j % 2 + 1))
            blocks.append(whole[i // 2, j // 2][rows, lanes])
    first = lax.axis_index("gx") % 2 == 0
    for n in range(5):
        rows = slice(128 * n, 128 * (n + 1))
        mine_ref[rows, :] = jnp.where(first, blocks[n], blocks[n + 5])
        other_ref[rows, :] = jnp.where(first, blocks[n + 5], blocks[n])
    copy.wait()


def plane_gram(received, grams, start_species):
    half = jax.ShapeDtypeStruct((640, 128), F32)
    whole = pl.BlockSpec(memory_space=pltpu.VMEM)
    return pl.pallas_call(
        plane_gram_kernel,
        out_shape=(jax.ShapeDtypeStruct((SPARE, 512), F32), half, half),
        in_specs=[whole, whole, whole],
        out_specs=(pl.BlockSpec(memory_space=pltpu.HBM), whole, whole),
        scratch_shapes=[
            pltpu.VMEM((1024, 256), BF16),
            pltpu.VMEM((1024, 256), BF16),
            pltpu.VMEM((768, 1024), BF16),
            pltpu.VMEM((768, 1024), BF16),
            pltpu.VMEM((768, 256), F32),
            pltpu.VMEM((512, 512), F32),
            pltpu.SemaphoreType.DMA,
        ],
        compiler_params=grant(20),
    )(received, grams, start_species.T)


def core_kernel(
    mine_ref, other_ref, turned_hbm, start_ref, out_ref, peaks_ref, image_ref, turned_ref, sem
):
    copy = pltpu.make_async_copy(turned_hbm.at[pl.ds(0, 512)], turned_ref, sem)
    copy.start()
    first = lax.axis_index("gx") % 2 == 0
    blocks = {}
    n = 0
    for i in range(4):
        for j in range(i, 4):
            rows = slice(128 * (n % 5), 128 * (n % 5 + 1))
            mine, other = mine_ref[rows, :], other_ref[rows, :]
            blocks[i, j] = jnp.where(first, mine, other) if n < 5 else jnp.where(first, other, mine)
            if i != j:
                blocks[j, i] = blocks[i, j].T
            n += 1
    gram = jnp.concatenate(
        [jnp.concatenate([blocks[i, j] for j in range(4)], axis=1) for i in range(4)], axis=0
    )
    basis = subspace(gram, start_ref[...], image_ref)
    copy.wait()
    th, tl = split2(turned_ref[...].T)
    bh, bl = split2(basis)
    core = bf16_dot(th, bh) + bf16_dot(th, bl) + bf16_dot(tl, bh)
    for r in range(16):
        out_ref[pl.ds(r, 24, stride=16), :] = core[32 * r : 32 * r + 24, :]
    peaks = jnp.max(jnp.abs(core).reshape(16, 32, 128), axis=2)
    peaks_ref[...] = peaks[:, 0:24]


def core_of(mine, other, turned, start_plane):
    whole = pl.BlockSpec(memory_space=pltpu.VMEM)
    return pl.pallas_call(
        core_kernel,
        out_shape=(jax.ShapeDtypeStruct((384, 128), F32), jax.ShapeDtypeStruct((16, 24), F32)),
        in_specs=[whole, whole, pl.BlockSpec(memory_space=pltpu.HBM), whole],
        scratch_shapes=[pltpu.VMEM((512, 128), F32), pltpu.VMEM((512, 512), F32), pltpu.SemaphoreType.DMA],
        compiler_params=grant(20),
    )(mine, other, turned, start_plane)


def over_plane(x):
    return lax.all_to_all(x, "gx", 0, 0, tiled=True, axis_index_groups=PLANES)


def copies(x, count):
    return jnp.broadcast_to(x[None], (count,) + x.shape)


def per_device(tensor, start_species, start_plane):
    sent = cells_first(tensor).reshape(256, 24, 128)
    received = lax.all_to_all(sent, BOTH, 0, 0, tiled=True).reshape(8, 768, 128)
    grams = species_gram(received)
    grams = grams + lax.ppermute(grams, "gx", PAIR)
    grams = jnp.sum(lax.all_to_all(copies(grams, 8), "sp", 0, 0, tiled=True), axis=0)
    grams = over_plane(copies(grams, 16))
    turned, mine, other = plane_gram(received, grams, start_species)
    mine = mine + lax.ppermute(other, "gx", PAIR)
    share = jnp.sum(over_plane(mine.reshape(16, 40, 128)), axis=0)
    share = jnp.sum(lax.all_to_all(copies(share, 8), "sp", 0, 0, tiled=True), axis=0)
    mine = over_plane(copies(share, 16)).reshape(640, 128)
    other = lax.ppermute(mine, "gx", PAIR)
    core_block, block_peaks = core_of(mine, other, turned, start_plane)
    return core_block.reshape(24, 16, 128), block_peaks.T


def solution(mesh):
    placed = (P("sp", "gx", None), P(), P())
    return jax.shard_map(
        per_device,
        mesh=mesh,
        in_specs=placed,
        out_specs=(P(BOTH, None, None), P(BOTH, None)),
        check_vma=False,
    )
```

```python
import jax
import jax.numpy as jnp
from jax import lax
from jax.experimental import pallas as pl
from jax.experimental.pallas import tpu as pltpu
from jax.sharding import PartitionSpec as P

SWEEPS = 4
CHUNKS = 4
SPARE = 32768
F32 = jnp.float32
BF16 = jnp.bfloat16
BOTH = ("sp", "gx")
NN = (((1,), (0,)), ((), ()))
NT = (((1,), (1,)), ((), ()))
TN = (((0,), (0,)), ((), ()))
PAIR = [(d, d ^ 1) for d in range(32)]
PLANES = [[d + core for d in range(0, 32, 2)] for core in range(2)]


def grant(mebibytes):
    return pltpu.CompilerParams(vmem_limit_bytes=mebibytes * 1024 * 1024)


def exact_dot(a, b, dims=NN):
    return lax.dot_general(a, b, dims, precision=lax.Precision.HIGHEST, preferred_element_type=F32)


def bf16_dot(a, b, dims=NN):
    return lax.dot_general(a, b, dims, preferred_element_type=F32)


def split2(x):
    high = x.astype(BF16)
    return high, (x - high.astype(F32)).astype(BF16)


def split3(x):
    high = x.astype(BF16)
    rest = x - high.astype(F32)
    mid = rest.astype(BF16)
    return high, mid, (rest - mid.astype(F32)).astype(BF16)


def six(a, b, dims=NN):
    (ah, am, al), (bh, bm, bl) = a, b
    (ka,), (kb,) = dims[0]
    n = bh.shape[1 - kb]
    left = jnp.concatenate([ah, am], axis=ka)
    right = jnp.concatenate([jnp.concatenate([x, x], axis=kb) for x in (bh, bm)], axis=1 - kb)
    main = bf16_dot(left, right, dims)
    rest = bf16_dot(jnp.concatenate([al, ah], axis=ka), jnp.concatenate([bh, bl], axis=kb), dims)
    return main[:, :n] + (main[:, n:] + rest)


def six_gram(a):
    high, mid, low = a
    left = jnp.concatenate([high, mid, low], axis=1)
    got = bf16_dot(left, jnp.concatenate([high, mid], axis=1), TN)
    small = got[256:384, 0:128] + bf16_dot(high, low, TN)
    cross = got[0:128, 128:256] + got[128:256, 0:128]
    return got[0:128, 0:128] + (cross + (got[128:256, 128:256] + small))


def across(x, j):
    return jnp.broadcast_to(x[:, j : j + 1], (8, 128))


def full_row(x, i):
    return jnp.broadcast_to(x[i : i + 1, :], (8, 128))


def inverse_factor(tiles, between=None):
    count = len(tiles)
    sub = lax.broadcasted_iota(jnp.int32, (8, 128), 0)
    lane = lax.broadcasted_iota(jnp.int32, (8, 128), 1)
    state = list(tiles)
    result = []
    for p in range(0, count, 2):
        at = 8 * p
        own_a, own_b = (lane >= at) & (lane < at + 8), (lane >= at + 8) & (lane < at + 16)
        unit_a = jnp.where(lane == sub + at, 1.0, 0.0)
        unit_b = jnp.where(lane == sub + at + 8, 1.0, 0.0)
        cols = [across(state[p], at + j) for j in range(8)]
        below = [across(state[p + 1], at + j) for j in range(8)]
        right = [across(state[p + 1], at + 8 + j) for j in range(8)]
        top = jnp.where(own_a, unit_a, state[p])
        low = jnp.where(own_a, 0.0, state[p + 1])
        diag = full_row(cols[0], 0)
        for j in range(8):
            recip = 1.0 / diag
            pivots = [full_row(cols[k], j) for k in range(j + 1, 8)]
            crossing = [full_row(below[j], k) for k in range(8)]
            if j < 7:
                diag = full_row(cols[j + 1], j + 1) - (full_row(cols[j], j + 1) * pivots[0]) * recip
            else:
                diag = full_row(right[0], 0) - (crossing[0] * crossing[0]) * recip
            root_a = recip if j == 0 else jnp.where(sub == j, recip, root_a)
            up = jnp.where(sub == j, 0.0, cols[j] * recip)
            down = below[j] * recip
            for k in range(j + 1, 8):
                cols[k] = cols[k] - up * pivots[k - j - 1]
                below[k] = below[k] - down * pivots[k - j - 1]
            for k in range(8):
                right[k] = right[k] - down * crossing[k]
            forward_a = top if j == 0 else jnp.where(sub == j, top, forward_a)
            pivot = full_row(top, j)
            top, low = top - up * pivot, low - down * pivot
        top = top * root_a
        mixed = [across(top, at + 8 + k) for k in range(8)]
        top = jnp.where(own_b, 0.0, top)
        low = jnp.where(own_b, unit_b, low)
        for j in range(8):
            recip = 1.0 / diag
            pivots = [full_row(right[k], j) for k in range(j + 1, 8)]
            if j < 7:
                diag = full_row(right[j + 1], j + 1) - (full_row(right[j], j + 1) * pivots[0]) * recip
            root_b = recip if j == 0 else jnp.where(sub == j, recip, root_b)
            up = jnp.where(sub == j, 0.0, right[j] * recip)
            for k in range(j + 1, 8):
                right[k] = right[k] - up * pivots[k - j - 1]
            forward_b = low if j == 0 else jnp.where(sub == j, low, forward_b)
            low = low - up * full_row(low, j)
        low = low * root_b
        result.append(jnp.where(lane < at + 8, forward_a * jnp.sqrt(root_a), 0.0))
        result.append(jnp.where(lane < at + 16, forward_b * jnp.sqrt(root_b), 0.0))
        low_rows = [full_row(low, k) for k in range(8)]
        for k in range(8):
            top = top - mixed[k] * low_rows[k]
        own = own_a | own_b
        near = min(p + 4, count)
        for k in range(p + 2, near):
            one = jnp.where(own, 0.0, state[k])
            for j in range(8):
                one = one - across(state[k], at + 8 + j) * low_rows[j]
            two = across(state[k], at) * full_row(top, 0)
            for j in range(1, 8):
                two = two + across(state[k], at + j) * full_row(top, j)
            state[k] = one - two
        if near < count:
            far = jnp.concatenate(state[near:], axis=0)
            ends = [jnp.zeros((8 * n, 128), F32) for n in (p, 14 - p)]
            weights = jnp.concatenate(([ends[0]] if p else []) + [top, low, ends[1]], axis=0)
            change = six(split3(far), split3(weights))
            for k in range(near, count):
                rows = slice(8 * (k - near), 8 * (k - near) + 8)
                state[k] = jnp.where(own, 0.0, state[k]) - change[rows]
        if between is not None:
            between(p // 2)
    return result


def subspace(gram, start, image_ref, aside):
    split_gram = split3(gram)
    image_block = six(split_gram, split3(start))
    chunk = gram.shape[0] // CHUNKS
    for sweep in range(SWEEPS):
        pieces = split3(image_block)
        inner = six_gram(pieces)
        last = sweep + 1 == SWEEPS

        def ahead(panel):
            aside(sweep, panel)
            if panel < CHUNKS and not last:
                rows = slice(chunk * panel, chunk * (panel + 1))
                image_ref[rows, :] = six(tuple(g[rows] for g in split_gram), pieces)

        tiles = [inner[8 * p : 8 * p + 8] for p in range(16)]
        factor = split3(jnp.concatenate(inverse_factor(tiles, ahead), axis=0))
        image_block = six(pieces if last else split3(image_ref[...]), factor, NT)
    return image_block


def subspace_narrow(gram, start, between):
    split_gram = split3(gram)
    image_block = six(split_gram, split3(start))
    blank = jnp.zeros((112, 128), F32)
    for sweep in range(SWEEPS):
        pieces = split3(image_block)
        inner = six_gram(pieces)
        ahead = pieces if sweep + 1 == SWEEPS else split3(six(split_gram, pieces))
        between(sweep)
        factor = inverse_factor([inner[0:8], inner[8:16]])
        image_block = six(ahead, split3(jnp.concatenate(factor + [blank], axis=0)), NT)
    return image_block


STEPS = 8


def cells_first_kernel(x_ref, o_ref, tile_ref, sems):
    step = o_ref.shape[0] // STEPS
    loads = [pltpu.make_async_copy(x_ref.at[:, pl.ds(step * k, step)], tile_ref.at[k], sems.at[k]) for k in range(STEPS)]
    for load in loads:
        load.start()
    for k in range(STEPS):
        loads[k].wait()
        for n in range(step // 128):
            tile = tile_ref[k, :, 128 * n : 128 * (n + 1)].reshape(8, 16, 128)
            rows = jnp.concatenate([tile[:, x, :] for x in range(16)], axis=0)
            at = step * k + 128 * n
            o_ref[at : at + 128, :] = rows.T


def cells_first(block):
    cells = block.shape[2]
    step = cells // STEPS
    return pl.pallas_call(
        cells_first_kernel,
        out_shape=jax.ShapeDtypeStruct((cells, 128), F32),
        in_specs=[pl.BlockSpec(memory_space=pltpu.HBM)],
        out_specs=pl.BlockSpec(memory_space=pltpu.VMEM),
        scratch_shapes=[pltpu.VMEM((STEPS, 128, step), F32), pltpu.SemaphoreType.DMA((STEPS,))],
        compiler_params=grant(50),
    )(block.reshape(128, cells))


def species_gram_kernel(r_ref, o_ref, ht_ref, h_ref, l_ref):
    for s in range(8):
        high, low = split2(r_ref[s])
        ht_ref[128 * s : 128 * (s + 1), :] = high.T
        h_ref[:, 128 * s : 128 * (s + 1)] = high
        l_ref[:, 128 * s : 128 * (s + 1)] = low
    lane = lax.broadcasted_iota(jnp.int32, (8, 256), 1) % 128
    rows = []
    for a in range(4):
        left = ht_ref[256 * a : 256 * (a + 1), :]
        parts = [[], []]
        for b in range(4):
            right = slice(256 * b, 256 * (b + 1))
            prod = bf16_dot(left, l_ref[:, right])
            if b >= a:
                main = bf16_dot(left, h_ref[:, right])
                prod = prod + (main if b > a else 0.5 * main)
            for half in range(2):
                acc = prod[128 * half : 128 * half + 8]
                for x in range(1, 16):
                    acc = jnp.where(lane // 8 == x, prod[128 * half + 8 * x : 128 * half + 8 * x + 8], acc)
                parts[half].append(acc)
        for half in range(2):
            rows.append(jnp.concatenate(parts[half], axis=1))
    wide = jnp.concatenate(rows, axis=0)
    fold = jnp.where(
        lax.broadcasted_iota(jnp.int32, (1024, 64), 0) // 128 * 8
        + lax.broadcasted_iota(jnp.int32, (1024, 64), 0) % 8
        == lax.broadcasted_iota(jnp.int32, (1024, 64), 1),
        1.0,
        0.0,
    ).astype(F32)
    half = exact_dot(wide, fold)
    gram = half + half.T
    second = jnp.concatenate([gram[48:64, 48:64], gram[16:32, 16:64]], axis=1)
    rows = jnp.concatenate([gram[0:16], second, gram[32:48]], axis=0)
    o_ref[...] = jnp.concatenate([rows[0:24], rows[24:48]], axis=1)


def species_gram(received):
    return pl.pallas_call(
        species_gram_kernel,
        out_shape=jax.ShapeDtypeStruct((24, 128), F32),
        scratch_shapes=[
            pltpu.VMEM((1024, 768), BF16),
            pltpu.VMEM((768, 1024), BF16),
            pltpu.VMEM((768, 1024), BF16),
        ],
        compiler_params=grant(16),
    )(received)


def plane_gram_kernel(
    r_ref, g_ref, start_ref, out_ref, mine_ref, other_ref, wh_ref, wl_ref, h_ref, l_ref, red_ref, turned_ref, sem
):
    def between(sweep):
        for s in (2 * sweep, 2 * sweep + 1):
            lanes = slice(128 * s, 128 * (s + 1))
            h_ref[:, lanes], l_ref[:, lanes] = split2(r_ref[s])

    folded = jnp.sum(g_ref[...], axis=0)
    rows = jnp.concatenate([folded[:, 0:64], folded[:, 64:128]], axis=0)
    across_rows = jnp.concatenate(
        [jnp.concatenate([rows, jnp.zeros((80, 64), F32)], axis=0), jnp.zeros((128, 64), F32)], axis=1
    ).T
    second = jnp.concatenate([across_rows[16:32, 0:16], rows[16:32, 16:64]], axis=1)
    last = jnp.concatenate([across_rows[48:64, 0:48], rows[16:32, 0:16]], axis=1)
    gram = jnp.concatenate([rows[0:16], second, rows[32:48], last], axis=0)
    start = jnp.concatenate([start_ref[...], jnp.zeros((112, 64), F32)], axis=0).T
    basis = subspace_narrow(gram, start, between)[:, 0:16]
    column = lax.broadcasted_iota(jnp.int32, (16, 256), 1)
    widen = jnp.where(
        column // 16 % 4 * 4 + column // 64 == lax.broadcasted_iota(jnp.int32, (16, 256), 0), 1.0, 0.0
    ).astype(BF16)
    high, mid, low = split3(basis)
    wide = bf16_dot(jnp.concatenate([high, mid, low], axis=1), jnp.concatenate([widen] * 3, axis=0))
    keep = (
        lax.broadcasted_iota(jnp.int32, (128, 256), 0) // 8 == lax.broadcasted_iota(jnp.int32, (128, 256), 1) % 16
    )
    for s in range(8):
        weights = jnp.where(keep, jnp.concatenate([wide[8 * s : 8 * s + 8]] * 16, axis=0), 0.0)
        high, low = split2(weights)
        wh_ref[128 * s : 128 * (s + 1), :] = high
        wl_ref[128 * s : 128 * (s + 1), :] = low
    wh = wh_ref[...]
    total = bf16_dot(h_ref[...], wh) + (bf16_dot(h_ref[...], wl_ref[...]) + bf16_dot(l_ref[...], wh))
    red_ref[...] = total
    lane = lax.broadcasted_iota(jnp.int32, (24, 128), 1)
    blank = jnp.zeros((8, 128), F32)
    for pair in range(16):
        rows = []
        for k in range(4):
            lanes = slice(128 * (k // 2), 128 * (k // 2 + 1))
            at = 48 * pair
            first, second = red_ref[at : at + 24, lanes], red_ref[at + 24 : at + 48, lanes]
            if k % 2:
                first = pltpu.roll(first, 64, 1)
            else:
                second = pltpu.roll(second, 64, 1)
            rows += [jnp.where(lane < 64, first, second), blank]
        turned = jnp.concatenate(rows, axis=0).T
        for g in range(2):
            for q in range(4):
                at, to = 64 * g + 16 * q, 32 * pair + 16 * g
                turned_ref[to : to + 16, 128 * q : 128 * (q + 1)] = turned[at : at + 16]
    copy = pltpu.make_async_copy(turned_ref, out_ref.at[pl.ds(0, 512)], sem)
    copy.start()
    high, low = split2(turned_ref[...])
    left = jnp.concatenate([high, high, low], axis=1)
    right = jnp.concatenate([high, low, high], axis=1)
    quarter = [slice(0, 256), slice(256, 512)]
    whole = {
        (i, j): bf16_dot(left[quarter[i]], right[quarter[j]], NT) for i, j in ((0, 0), (0, 1), (1, 1))
    }
    blocks = []
    for i in range(4):
        for j in range(i, 4):
            rows, lanes = slice(128 * (i % 2), 128 * (i % 2 + 1)), slice(128 * (j % 2), 128 * (j % 2 + 1))
            blocks.append(whole[i // 2, j // 2][rows, lanes])
    first = lax.axis_index("gx") % 2 == 0
    for n in range(5):
        rows = slice(128 * n, 128 * (n + 1))
        mine_ref[rows, :] = jnp.where(first, blocks[n], blocks[n + 5])
        other_ref[rows, :] = jnp.where(first, blocks[n + 5], blocks[n])
    copy.wait()


def plane_gram(received, grams, start_species):
    half = jax.ShapeDtypeStruct((640, 128), F32)
    whole = pl.BlockSpec(memory_space=pltpu.VMEM)
    return pl.pallas_call(
        plane_gram_kernel,
        out_shape=(jax.ShapeDtypeStruct((SPARE, 512), F32), half, half),
        in_specs=[whole, whole, whole],
        out_specs=(pl.BlockSpec(memory_space=pltpu.HBM), whole, whole),
        scratch_shapes=[
            pltpu.VMEM((1024, 256), BF16),
            pltpu.VMEM((1024, 256), BF16),
            pltpu.VMEM((768, 1024), BF16),
            pltpu.VMEM((768, 1024), BF16),
            pltpu.VMEM((768, 256), F32),
            pltpu.VMEM((512, 512), F32),
            pltpu.SemaphoreType.DMA,
        ],
        compiler_params=grant(20),
    )(received, grams, start_species.T)


def core_kernel(
    mine_ref, other_ref, turned_hbm, start_ref, out_ref, peaks_ref, image_ref, turned_ref, high_ref, low_ref, sem
):
    copy = pltpu.make_async_copy(turned_hbm.at[pl.ds(0, 512)], turned_ref, sem)
    copy.start()
    first = lax.axis_index("gx") % 2 == 0
    blocks = {}
    n = 0
    for i in range(4):
        for j in range(i, 4):
            rows = slice(128 * (n % 5), 128 * (n % 5 + 1))
            mine, other = mine_ref[rows, :], other_ref[rows, :]
            blocks[i, j] = jnp.where(first, mine, other) if n < 5 else jnp.where(first, other, mine)
            if i != j:
                blocks[j, i] = blocks[i, j].T
            n += 1
    gram = jnp.concatenate(
        [jnp.concatenate([blocks[i, j] for j in range(4)], axis=1) for i in range(4)], axis=0
    )

    def aside(sweep, panel):
        if sweep == 1 and panel < 4:
            if panel == 0:
                copy.wait()
            lanes = slice(128 * panel, 128 * (panel + 1))
            high_ref[:, lanes], low_ref[:, lanes] = split2(turned_ref[lanes, :].T)

    basis = subspace(gram, start_ref[...], image_ref, aside)
    bh, bl = split2(basis)
    wide = bf16_dot(high_ref[...], jnp.concatenate([bh, bl], axis=1))
    core = wide[:, 0:128] + (wide[:, 128:256] + bf16_dot(low_ref[...], bh))
    for r in range(16):
        out_ref[pl.ds(r, 24, stride=16), :] = core[32 * r : 32 * r + 24, :]
    peaks = jnp.max(jnp.abs(core).reshape(16, 32, 128), axis=2)
    peaks_ref[...] = peaks[:, 0:24]


def core_of(mine, other, turned, start_plane):
    whole = pl.BlockSpec(memory_space=pltpu.VMEM)
    return pl.pallas_call(
        core_kernel,
        out_shape=(jax.ShapeDtypeStruct((384, 128), F32), jax.ShapeDtypeStruct((16, 24), F32)),
        in_specs=[whole, whole, pl.BlockSpec(memory_space=pltpu.HBM), whole],
        scratch_shapes=[
            pltpu.VMEM((512, 128), F32),
            pltpu.VMEM((512, 512), F32),
            pltpu.VMEM((512, 512), BF16),
            pltpu.VMEM((512, 512), BF16),
            pltpu.SemaphoreType.DMA,
        ],
        compiler_params=grant(20),
    )(mine, other, turned, start_plane)


def over_plane(x):
    return lax.all_to_all(x, "gx", 0, 0, tiled=True, axis_index_groups=PLANES)


def copies(x, count):
    return jnp.broadcast_to(x[None], (count,) + x.shape)


def per_device(tensor, start_species, start_plane):
    sent = cells_first(tensor).reshape(256, 24, 128)
    received = lax.all_to_all(sent, BOTH, 0, 0, tiled=True).reshape(8, 768, 128)
    grams = species_gram(received)
    grams = grams + lax.ppermute(grams, "gx", PAIR)
    grams = jnp.sum(lax.all_to_all(copies(grams, 8), "sp", 0, 0, tiled=True), axis=0)
    grams = over_plane(copies(grams, 16))
    turned, mine, other = plane_gram(received, grams, start_species)
    mine = mine + lax.ppermute(other, "gx", PAIR)
    share = jnp.sum(over_plane(mine.reshape(16, 40, 128)), axis=0)
    share = jnp.sum(lax.all_to_all(copies(share, 8), "sp", 0, 0, tiled=True), axis=0)
    mine = over_plane(copies(share, 16)).reshape(640, 128)
    other = lax.ppermute(mine, "gx", PAIR)
    core_block, block_peaks = core_of(mine, other, turned, start_plane)
    return core_block.reshape(24, 16, 128), block_peaks.T


def solution(mesh):
    placed = (P("sp", "gx", None), P(), P())
    return jax.shard_map(
        per_device,
        mesh=mesh,
        in_specs=placed,
        out_specs=(P(BOTH, None, None), P(BOTH, None)),
        check_vma=False,
    )
```

```python
import jax
import jax.numpy as jnp
from jax import lax
from jax.experimental import pallas as pl
from jax.experimental.pallas import tpu as pltpu
from jax.sharding import PartitionSpec as P

SWEEPS = 4
CHUNKS = 4
SPARE = 32768
F32 = jnp.float32
BF16 = jnp.bfloat16
BOTH = ("sp", "gx")
NN = (((1,), (0,)), ((), ()))
NT = (((1,), (1,)), ((), ()))
TN = (((0,), (0,)), ((), ()))
PAIR = [(d, d ^ 1) for d in range(32)]
PLANES = [[d + core for d in range(0, 32, 2)] for core in range(2)]


def grant(mebibytes):
    return pltpu.CompilerParams(vmem_limit_bytes=mebibytes * 1024 * 1024)


def exact_dot(a, b, dims=NN):
    return lax.dot_general(a, b, dims, precision=lax.Precision.HIGHEST, preferred_element_type=F32)


def bf16_dot(a, b, dims=NN):
    return lax.dot_general(a, b, dims, preferred_element_type=F32)


def split2(x):
    high = x.astype(BF16)
    return high, (x - high.astype(F32)).astype(BF16)


def split3(x):
    high = x.astype(BF16)
    rest = x - high.astype(F32)
    mid = rest.astype(BF16)
    return high, mid, (rest - mid.astype(F32)).astype(BF16)


def six(a, b, dims=NN):
    (ah, am, al), (bh, bm, bl) = a, b
    (ka,), (kb,) = dims[0]
    n = bh.shape[1 - kb]
    left = jnp.concatenate([ah, am], axis=ka)
    right = jnp.concatenate([jnp.concatenate([x, x], axis=kb) for x in (bh, bm)], axis=1 - kb)
    main = bf16_dot(left, right, dims)
    rest = bf16_dot(jnp.concatenate([al, ah], axis=ka), jnp.concatenate([bh, bl], axis=kb), dims)
    return main[:, :n] + (main[:, n:] + rest)


def six_gram(a):
    high, mid, low = a
    left = jnp.concatenate([high, mid, low], axis=1)
    got = bf16_dot(left, jnp.concatenate([high, mid], axis=1), TN)
    small = got[256:384, 0:128] + bf16_dot(high, low, TN)
    cross = got[0:128, 128:256] + got[128:256, 0:128]
    return got[0:128, 0:128] + (cross + (got[128:256, 128:256] + small))


def across(x, j):
    return jnp.broadcast_to(x[:, j : j + 1], (8, 128))


def full_row(x, i):
    return jnp.broadcast_to(x[i : i + 1, :], (8, 128))


def inverse_factor(tiles, between=None):
    count = len(tiles)
    sub = lax.broadcasted_iota(jnp.int32, (8, 128), 0)
    lane = lax.broadcasted_iota(jnp.int32, (8, 128), 1)
    state = list(tiles)
    result = []
    for p in range(0, count, 2):
        at = 8 * p
        own_a, own_b = (lane >= at) & (lane < at + 8), (lane >= at + 8) & (lane < at + 16)
        unit_a = jnp.where(lane == sub + at, 1.0, 0.0)
        unit_b = jnp.where(lane == sub + at + 8, 1.0, 0.0)
        cols = [across(state[p], at + j) for j in range(8)]
        below = [across(state[p + 1], at + j) for j in range(8)]
        right = [across(state[p + 1], at + 8 + j) for j in range(8)]
        top = jnp.where(own_a, unit_a, state[p])
        low = jnp.where(own_a, 0.0, state[p + 1])
        diag = full_row(cols[0], 0)
        for j in range(8):
            recip = 1.0 / diag
            pivots = [full_row(cols[k], j) for k in range(j + 1, 8)]
            crossing = [full_row(below[j], k) for k in range(8)]
            if j < 7:
                diag = full_row(cols[j + 1], j + 1) - (full_row(cols[j], j + 1) * pivots[0]) * recip
            else:
                diag = full_row(right[0], 0) - (crossing[0] * crossing[0]) * recip
            root_a = recip if j == 0 else jnp.where(sub == j, recip, root_a)
            up = jnp.where(sub == j, 0.0, cols[j] * recip)
            down = below[j] * recip
            for k in range(j + 1, 8):
                cols[k] = cols[k] - up * pivots[k - j - 1]
                below[k] = below[k] - down * pivots[k - j - 1]
            for k in range(8):
                right[k] = right[k] - down * crossing[k]
            forward_a = top if j == 0 else jnp.where(sub == j, top, forward_a)
            pivot = full_row(top, j)
            top, low = top - up * pivot, low - down * pivot
        top = top * root_a
        mixed = [across(top, at + 8 + k) for k in range(8)]
        top = jnp.where(own_b, 0.0, top)
        low = jnp.where(own_b, unit_b, low)
        for j in range(8):
            recip = 1.0 / diag
            pivots = [full_row(right[k], j) for k in range(j + 1, 8)]
            if j < 7:
                diag = full_row(right[j + 1], j + 1) - (full_row(right[j], j + 1) * pivots[0]) * recip
            root_b = recip if j == 0 else jnp.where(sub == j, recip, root_b)
            up = jnp.where(sub == j, 0.0, right[j] * recip)
            for k in range(j + 1, 8):
                right[k] = right[k] - up * pivots[k - j - 1]
            forward_b = low if j == 0 else jnp.where(sub == j, low, forward_b)
            low = low - up * full_row(low, j)
        low = low * root_b
        result.append(jnp.where(lane < at + 8, forward_a * jnp.sqrt(root_a), 0.0))
        result.append(jnp.where(lane < at + 16, forward_b * jnp.sqrt(root_b), 0.0))
        low_rows = [full_row(low, k) for k in range(8)]
        for k in range(8):
            top = top - mixed[k] * low_rows[k]
        own = own_a | own_b
        near = min(p + 4, count)
        for k in range(p + 2, near):
            one = jnp.where(own, 0.0, state[k])
            for j in range(8):
                one = one - across(state[k], at + 8 + j) * low_rows[j]
            two = across(state[k], at) * full_row(top, 0)
            for j in range(1, 8):
                two = two + across(state[k], at + j) * full_row(top, j)
            state[k] = one - two
        if near < count:
            far = jnp.concatenate(state[near:], axis=0)
            ends = [jnp.zeros((8 * n, 128), F32) for n in (p, 14 - p)]
            weights = jnp.concatenate(([ends[0]] if p else []) + [top, low, ends[1]], axis=0)
            change = six(split3(far), split3(weights))
            for k in range(near, count):
                rows = slice(8 * (k - near), 8 * (k - near) + 8)
                state[k] = jnp.where(own, 0.0, state[k]) - change[rows]
        if between is not None:
            between(p // 2)
    return result


def subspace(gram, start, image_ref, aside):
    split_gram = split3(gram)
    image_block = six(split_gram, split3(start))
    chunk = gram.shape[0] // CHUNKS
    for sweep in range(SWEEPS):
        pieces = split3(image_block)
        inner = six_gram(pieces)
        last = sweep + 1 == SWEEPS

        def ahead(panel):
            aside(sweep, panel)
            if panel < CHUNKS and not last:
                rows = slice(chunk * panel, chunk * (panel + 1))
                image_ref[rows, :] = six(tuple(g[rows] for g in split_gram), pieces)

        tiles = [inner[8 * p : 8 * p + 8] for p in range(16)]
        factor = split3(jnp.concatenate(inverse_factor(tiles, ahead), axis=0))
        image_block = six(pieces if last else split3(image_ref[...]), factor, NT)
    return image_block


def subspace_narrow(gram, start, between):
    split_gram = split3(gram)
    image_block = six(split_gram, split3(start))
    blank = jnp.zeros((112, 128), F32)
    for sweep in range(SWEEPS):
        pieces = split3(image_block)
        inner = six_gram(pieces)
        ahead = pieces if sweep + 1 == SWEEPS else split3(six(split_gram, pieces))
        between(sweep)
        factor = inverse_factor([inner[0:8], inner[8:16]])
        image_block = six(ahead, split3(jnp.concatenate(factor + [blank], axis=0)), NT)
    return image_block


STEPS = 8


def cells_first_kernel(x_ref, o_ref, tile_ref, sems):
    step = o_ref.shape[0] // STEPS
    loads = [pltpu.make_async_copy(x_ref.at[:, pl.ds(step * k, step)], tile_ref.at[k], sems.at[k]) for k in range(STEPS)]
    for load in loads:
        load.start()
    for k in range(STEPS):
        loads[k].wait()
        for n in range(step // 128):
            tile = tile_ref[k, :, 128 * n : 128 * (n + 1)].reshape(8, 16, 128)
            rows = jnp.concatenate([tile[:, x, :] for x in range(16)], axis=0)
            at = step * k + 128 * n
            o_ref[at : at + 128, :] = rows.T


def cells_first(block):
    cells = block.shape[2]
    step = cells // STEPS
    return pl.pallas_call(
        cells_first_kernel,
        out_shape=jax.ShapeDtypeStruct((cells, 128), F32),
        in_specs=[pl.BlockSpec(memory_space=pltpu.HBM)],
        out_specs=pl.BlockSpec(memory_space=pltpu.VMEM),
        scratch_shapes=[pltpu.VMEM((STEPS, 128, step), F32), pltpu.SemaphoreType.DMA((STEPS,))],
        compiler_params=grant(50),
    )(block.reshape(128, cells))


def species_gram_kernel(r_ref, o_ref, ht_ref, h_ref, l_ref):
    for s in range(8):
        high, low = split2(r_ref[s])
        ht_ref[128 * s : 128 * (s + 1), :] = high.T
        h_ref[:, 128 * s : 128 * (s + 1)] = high
        l_ref[:, 128 * s : 128 * (s + 1)] = low
    lane = lax.broadcasted_iota(jnp.int32, (8, 256), 1) % 128
    rows = []
    for a in range(4):
        left = ht_ref[256 * a : 256 * (a + 1), :]
        parts = [[], []]
        for b in range(4):
            right = slice(256 * b, 256 * (b + 1))
            prod = bf16_dot(left, l_ref[:, right])
            if b >= a:
                main = bf16_dot(left, h_ref[:, right])
                prod = prod + (main if b > a else 0.5 * main)
            for half in range(2):
                acc = prod[128 * half : 128 * half + 8]
                for x in range(1, 16):
                    acc = jnp.where(lane // 8 == x, prod[128 * half + 8 * x : 128 * half + 8 * x + 8], acc)
                parts[half].append(acc)
        for half in range(2):
            rows.append(jnp.concatenate(parts[half], axis=1))
    wide = jnp.concatenate(rows, axis=0)
    fold = jnp.where(
        lax.broadcasted_iota(jnp.int32, (1024, 64), 0) // 128 * 8
        + lax.broadcasted_iota(jnp.int32, (1024, 64), 0) % 8
        == lax.broadcasted_iota(jnp.int32, (1024, 64), 1),
        1.0,
        0.0,
    ).astype(F32)
    half = exact_dot(wide, fold)
    gram = half + half.T
    second = jnp.concatenate([gram[48:64, 48:64], gram[16:32, 16:64]], axis=1)
    rows = jnp.concatenate([gram[0:16], second, gram[32:48]], axis=0)
    o_ref[...] = jnp.concatenate([rows[0:24], rows[24:48]], axis=1)


def species_gram(received):
    return pl.pallas_call(
        species_gram_kernel,
        out_shape=jax.ShapeDtypeStruct((24, 128), F32),
        scratch_shapes=[
            pltpu.VMEM((1024, 768), BF16),
            pltpu.VMEM((768, 1024), BF16),
            pltpu.VMEM((768, 1024), BF16),
        ],
        compiler_params=grant(16),
    )(received)


def plane_gram_kernel(
    r_ref, g_ref, start_ref, out_ref, mine_ref, other_ref, wh_ref, wl_ref, h_ref, l_ref, red_ref, turned_ref, sem
):
    def between(sweep):
        for s in (2 * sweep, 2 * sweep + 1):
            lanes = slice(128 * s, 128 * (s + 1))
            h_ref[:, lanes], l_ref[:, lanes] = split2(r_ref[s])

    folded = jnp.sum(g_ref[...], axis=0)
    rows = jnp.concatenate([folded[:, 0:64], folded[:, 64:128]], axis=0)
    across_rows = jnp.concatenate(
        [jnp.concatenate([rows, jnp.zeros((80, 64), F32)], axis=0), jnp.zeros((128, 64), F32)], axis=1
    ).T
    second = jnp.concatenate([across_rows[16:32, 0:16], rows[16:32, 16:64]], axis=1)
    last = jnp.concatenate([across_rows[48:64, 0:48], rows[16:32, 0:16]], axis=1)
    gram = jnp.concatenate([rows[0:16], second, rows[32:48], last], axis=0)
    start = jnp.concatenate([start_ref[...], jnp.zeros((112, 64), F32)], axis=0).T
    basis = subspace_narrow(gram, start, between)[:, 0:16]
    column = lax.broadcasted_iota(jnp.int32, (16, 256), 1)
    widen = jnp.where(
        column // 16 % 4 * 4 + column // 64 == lax.broadcasted_iota(jnp.int32, (16, 256), 0), 1.0, 0.0
    ).astype(BF16)
    high, mid, low = split3(basis)
    wide = bf16_dot(jnp.concatenate([high, mid, low], axis=1), jnp.concatenate([widen] * 3, axis=0))
    keep = (
        lax.broadcasted_iota(jnp.int32, (128, 256), 0) // 8 == lax.broadcasted_iota(jnp.int32, (128, 256), 1) % 16
    )
    for s in range(8):
        weights = jnp.where(keep, jnp.concatenate([wide[8 * s : 8 * s + 8]] * 16, axis=0), 0.0)
        high, low = split2(weights)
        wh_ref[128 * s : 128 * (s + 1), :] = high
        wl_ref[128 * s : 128 * (s + 1), :] = low
    wh, wl = wh_ref[...], wl_ref[...]
    for n in range(2):
        rows = slice(384 * n, 384 * (n + 1))
        high = h_ref[rows, :]
        red_ref[rows, :] = bf16_dot(high, wh) + (bf16_dot(high, wl) + bf16_dot(l_ref[rows, :], wh))
    lane = lax.broadcasted_iota(jnp.int32, (24, 128), 1)
    blank = jnp.zeros((8, 128), F32)
    for pair in range(16):
        rows = []
        for k in range(4):
            lanes = slice(128 * (k // 2), 128 * (k // 2 + 1))
            at = 48 * pair
            first, second = red_ref[at : at + 24, lanes], red_ref[at + 24 : at + 48, lanes]
            if k % 2:
                first = pltpu.roll(first, 64, 1)
            else:
                second = pltpu.roll(second, 64, 1)
            rows += [jnp.where(lane < 64, first, second), blank]
        turned = jnp.concatenate(rows, axis=0).T
        for g in range(2):
            for q in range(4):
                at, to = 64 * g + 16 * q, 32 * pair + 16 * g
                turned_ref[to : to + 16, 128 * q : 128 * (q + 1)] = turned[at : at + 16]
    copy = pltpu.make_async_copy(turned_ref, out_ref.at[pl.ds(0, 512)], sem)
    copy.start()
    high, low = split2(turned_ref[...])
    left = jnp.concatenate([high, high, low], axis=1)
    right = jnp.concatenate([high, low, high], axis=1)
    quarter = [slice(0, 256), slice(256, 512)]
    whole = {
        (i, j): bf16_dot(left[quarter[i]], right[quarter[j]], NT) for i, j in ((0, 0), (0, 1), (1, 1))
    }
    blocks = []
    for i in range(4):
        for j in range(i, 4):
            rows, lanes = slice(128 * (i % 2), 128 * (i % 2 + 1)), slice(128 * (j % 2), 128 * (j % 2 + 1))
            blocks.append(whole[i // 2, j // 2][rows, lanes])
    first = lax.axis_index("gx") % 2 == 0
    for n in range(5):
        rows = slice(128 * n, 128 * (n + 1))
        mine_ref[rows, :] = jnp.where(first, blocks[n], blocks[n + 5])
        other_ref[rows, :] = jnp.where(first, blocks[n + 5], blocks[n])
    copy.wait()


def plane_gram(received, grams, start_species):
    half = jax.ShapeDtypeStruct((640, 128), F32)
    whole = pl.BlockSpec(memory_space=pltpu.VMEM)
    return pl.pallas_call(
        plane_gram_kernel,
        out_shape=(jax.ShapeDtypeStruct((SPARE, 512), F32), half, half),
        in_specs=[whole, whole, whole],
        out_specs=(pl.BlockSpec(memory_space=pltpu.HBM), whole, whole),
        scratch_shapes=[
            pltpu.VMEM((1024, 256), BF16),
            pltpu.VMEM((1024, 256), BF16),
            pltpu.VMEM((768, 1024), BF16),
            pltpu.VMEM((768, 1024), BF16),
            pltpu.VMEM((768, 256), F32),
            pltpu.VMEM((512, 512), F32),
            pltpu.SemaphoreType.DMA,
        ],
        compiler_params=grant(20),
    )(received, grams, start_species.T)


def core_kernel(
    mine_ref, other_ref, turned_hbm, start_ref, out_ref, peaks_ref, image_ref, turned_ref, high_ref, low_ref, sem
):
    copy = pltpu.make_async_copy(turned_hbm.at[pl.ds(0, 512)], turned_ref, sem)
    copy.start()
    first = lax.axis_index("gx") % 2 == 0
    blocks = {}
    n = 0
    for i in range(4):
        for j in range(i, 4):
            rows = slice(128 * (n % 5), 128 * (n % 5 + 1))
            mine, other = mine_ref[rows, :], other_ref[rows, :]
            blocks[i, j] = jnp.where(first, mine, other) if n < 5 else jnp.where(first, other, mine)
            if i != j:
                blocks[j, i] = blocks[i, j].T
            n += 1
    gram = jnp.concatenate(
        [jnp.concatenate([blocks[i, j] for j in range(4)], axis=1) for i in range(4)], axis=0
    )

    def aside(sweep, panel):
        if sweep == 1 and panel < 4:
            if panel == 0:
                copy.wait()
            lanes = slice(128 * panel, 128 * (panel + 1))
            high_ref[:, lanes], low_ref[:, lanes] = split2(turned_ref[lanes, :].T)

    basis = subspace(gram, start_ref[...], image_ref, aside)
    bh, bl = split2(basis)
    wide = bf16_dot(high_ref[...], jnp.concatenate([bh, bl], axis=1))
    core = wide[:, 0:128] + (wide[:, 128:256] + bf16_dot(low_ref[...], bh))
    for r in range(16):
        out_ref[pl.ds(r, 24, stride=16), :] = core[32 * r : 32 * r + 24, :]
    peaks = jnp.max(jnp.abs(core).reshape(16, 32, 128), axis=2)
    peaks_ref[...] = peaks[:, 0:24]


def core_of(mine, other, turned, start_plane):
    whole = pl.BlockSpec(memory_space=pltpu.VMEM)
    return pl.pallas_call(
        core_kernel,
        out_shape=(jax.ShapeDtypeStruct((384, 128), F32), jax.ShapeDtypeStruct((16, 24), F32)),
        in_specs=[whole, whole, pl.BlockSpec(memory_space=pltpu.HBM), whole],
        scratch_shapes=[
            pltpu.VMEM((512, 128), F32),
            pltpu.VMEM((512, 512), F32),
            pltpu.VMEM((512, 512), BF16),
            pltpu.VMEM((512, 512), BF16),
            pltpu.SemaphoreType.DMA,
        ],
        compiler_params=grant(20),
    )(mine, other, turned, start_plane)


def over_plane(x):
    return lax.all_to_all(x, "gx", 0, 0, tiled=True, axis_index_groups=PLANES)


def copies(x, count):
    return jnp.broadcast_to(x[None], (count,) + x.shape)


def per_device(tensor, start_species, start_plane):
    sent = cells_first(tensor).reshape(256, 24, 128)
    received = lax.all_to_all(sent, BOTH, 0, 0, tiled=True).reshape(8, 768, 128)
    grams = species_gram(received)
    grams = grams + lax.ppermute(grams, "gx", PAIR)
    grams = jnp.sum(lax.all_to_all(copies(grams, 8), "sp", 0, 0, tiled=True), axis=0)
    grams = over_plane(copies(grams, 16))
    turned, mine, other = plane_gram(received, grams, start_species)
    mine = mine + lax.ppermute(other, "gx", PAIR)
    share = jnp.sum(over_plane(mine.reshape(16, 40, 128)), axis=0)
    share = jnp.sum(lax.all_to_all(copies(share, 8), "sp", 0, 0, tiled=True), axis=0)
    mine = over_plane(copies(share, 16)).reshape(640, 128)
    other = lax.ppermute(mine, "gx", PAIR)
    core_block, block_peaks = core_of(mine, other, turned, start_plane)
    return core_block.reshape(24, 16, 128), block_peaks.T


def solution(mesh):
    placed = (P("sp", "gx", None), P(), P())
    return jax.shard_map(
        per_device,
        mesh=mesh,
        in_specs=placed,
        out_specs=(P(BOTH, None, None), P(BOTH, None)),
        check_vma=False,
    )
```

```python
import jax
import jax.numpy as jnp
from jax import lax
from jax.experimental import pallas as pl
from jax.experimental.pallas import tpu as pltpu
from jax.sharding import PartitionSpec as P

SWEEPS = 4
CHUNKS = 4
SPARE = 32768
F32 = jnp.float32
BF16 = jnp.bfloat16
BOTH = ("sp", "gx")
NN = (((1,), (0,)), ((), ()))
NT = (((1,), (1,)), ((), ()))
TN = (((0,), (0,)), ((), ()))
PAIR = [(d, d ^ 1) for d in range(32)]
PLANES = [[d + core for d in range(0, 32, 2)] for core in range(2)]


def grant(mebibytes):
    return pltpu.CompilerParams(vmem_limit_bytes=mebibytes * 1024 * 1024)


def exact_dot(a, b, dims=NN):
    return lax.dot_general(a, b, dims, precision=lax.Precision.HIGHEST, preferred_element_type=F32)


def bf16_dot(a, b, dims=NN):
    return lax.dot_general(a, b, dims, preferred_element_type=F32)


def split2(x):
    high = x.astype(BF16)
    return high, (x - high.astype(F32)).astype(BF16)


def split3(x):
    high = x.astype(BF16)
    rest = x - high.astype(F32)
    mid = rest.astype(BF16)
    return high, mid, (rest - mid.astype(F32)).astype(BF16)


def six(a, b, dims=NN):
    (ah, am, al), (bh, bm, bl) = a, b
    (ka,), (kb,) = dims[0]
    n = bh.shape[1 - kb]
    left = jnp.concatenate([ah, am], axis=ka)
    right = jnp.concatenate([jnp.concatenate([x, x], axis=kb) for x in (bh, bm)], axis=1 - kb)
    main = bf16_dot(left, right, dims)
    rest = bf16_dot(jnp.concatenate([al, ah], axis=ka), jnp.concatenate([bh, bl], axis=kb), dims)
    return main[:, :n] + (main[:, n:] + rest)


def six_gram(a):
    high, mid, low = a
    left = jnp.concatenate([high, mid, low], axis=1)
    got = bf16_dot(left, jnp.concatenate([high, mid], axis=1), TN)
    small = got[256:384, 0:128] + bf16_dot(high, low, TN)
    cross = got[0:128, 128:256] + got[128:256, 0:128]
    return got[0:128, 0:128] + (cross + (got[128:256, 128:256] + small))


def across(x, j):
    return jnp.broadcast_to(x[:, j : j + 1], (8, 128))


def full_row(x, i):
    return jnp.broadcast_to(x[i : i + 1, :], (8, 128))


def inverse_factor(tiles, between=None):
    count = len(tiles)
    sub = lax.broadcasted_iota(jnp.int32, (8, 128), 0)
    lane = lax.broadcasted_iota(jnp.int32, (8, 128), 1)
    state = list(tiles)
    result = []
    for p in range(0, count, 2):
        at = 8 * p
        own_a, own_b = (lane >= at) & (lane < at + 8), (lane >= at + 8) & (lane < at + 16)
        unit_a = jnp.where(lane == sub + at, 1.0, 0.0)
        unit_b = jnp.where(lane == sub + at + 8, 1.0, 0.0)
        cols = [across(state[p], at + j) for j in range(8)]
        below = [across(state[p + 1], at + j) for j in range(8)]
        right = [across(state[p + 1], at + 8 + j) for j in range(8)]
        top = jnp.where(own_a, unit_a, state[p])
        low = jnp.where(own_a, 0.0, state[p + 1])
        diag = full_row(cols[0], 0)
        for j in range(8):
            recip = 1.0 / diag
            pivots = [full_row(cols[k], j) for k in range(j + 1, 8)]
            crossing = [full_row(below[j], k) for k in range(8)]
            if j < 7:
                diag = full_row(cols[j + 1], j + 1) - (full_row(cols[j], j + 1) * pivots[0]) * recip
            else:
                diag = full_row(right[0], 0) - (crossing[0] * crossing[0]) * recip
            root_a = recip if j == 0 else jnp.where(sub == j, recip, root_a)
            up = jnp.where(sub == j, 0.0, cols[j] * recip)
            down = below[j] * recip
            for k in range(j + 1, 8):
                cols[k] = cols[k] - up * pivots[k - j - 1]
                below[k] = below[k] - down * pivots[k - j - 1]
            for k in range(8):
                right[k] = right[k] - down * crossing[k]
            forward_a = top if j == 0 else jnp.where(sub == j, top, forward_a)
            pivot = full_row(top, j)
            top, low = top - up * pivot, low - down * pivot
        top = top * root_a
        mixed = [across(top, at + 8 + k) for k in range(8)]
        top = jnp.where(own_b, 0.0, top)
        low = jnp.where(own_b, unit_b, low)
        for j in range(8):
            recip = 1.0 / diag
            pivots = [full_row(right[k], j) for k in range(j + 1, 8)]
            if j < 7:
                diag = full_row(right[j + 1], j + 1) - (full_row(right[j], j + 1) * pivots[0]) * recip
            root_b = recip if j == 0 else jnp.where(sub == j, recip, root_b)
            up = jnp.where(sub == j, 0.0, right[j] * recip)
            for k in range(j + 1, 8):
                right[k] = right[k] - up * pivots[k - j - 1]
            forward_b = low if j == 0 else jnp.where(sub == j, low, forward_b)
            low = low - up * full_row(low, j)
        low = low * root_b
        result.append(jnp.where(lane < at + 8, forward_a * jnp.sqrt(root_a), 0.0))
        result.append(jnp.where(lane < at + 16, forward_b * jnp.sqrt(root_b), 0.0))
        low_rows = [full_row(low, k) for k in range(8)]
        for k in range(8):
            top = top - mixed[k] * low_rows[k]
        own = own_a | own_b
        near = min(p + 4, count)
        for k in range(p + 2, near):
            one = jnp.where(own, 0.0, state[k])
            for j in range(8):
                one = one - across(state[k], at + 8 + j) * low_rows[j]
            two = across(state[k], at) * full_row(top, 0)
            for j in range(1, 8):
                two = two + across(state[k], at + j) * full_row(top, j)
            state[k] = one - two
        if near < count:
            far = jnp.concatenate(state[near:], axis=0)
            ends = [jnp.zeros((8 * n, 128), F32) for n in (p, 14 - p)]
            weights = jnp.concatenate(([ends[0]] if p else []) + [top, low, ends[1]], axis=0)
            change = six(split3(far), split3(weights))
            for k in range(near, count):
                rows = slice(8 * (k - near), 8 * (k - near) + 8)
                state[k] = jnp.where(own, 0.0, state[k]) - change[rows]
        if between is not None:
            between(p // 2)
    return result


def subspace(gram, start, image_ref, aside):
    split_gram = split3(gram)
    image_block = six(split_gram, split3(start))
    chunk = gram.shape[0] // CHUNKS
    for sweep in range(SWEEPS):
        pieces = split3(image_block)
        inner = six_gram(pieces)
        last = sweep + 1 == SWEEPS

        def ahead(panel):
            aside(sweep, panel)
            if panel < CHUNKS and not last:
                rows = slice(chunk * panel, chunk * (panel + 1))
                image_ref[rows, :] = six(tuple(g[rows] for g in split_gram), pieces)

        tiles = [inner[8 * p : 8 * p + 8] for p in range(16)]
        factor = split3(jnp.concatenate(inverse_factor(tiles, ahead), axis=0))
        image_block = six(pieces if last else split3(image_ref[...]), factor, NT)
    return image_block


def subspace_narrow(gram, start, between):
    split_gram = split3(gram)
    image_block = six(split_gram, split3(start))
    blank = jnp.zeros((112, 128), F32)
    for sweep in range(SWEEPS):
        pieces = split3(image_block)
        inner = six_gram(pieces)
        ahead = pieces if sweep + 1 == SWEEPS else split3(six(split_gram, pieces))
        between(sweep)
        factor = inverse_factor([inner[0:8], inner[8:16]])
        image_block = six(ahead, split3(jnp.concatenate(factor + [blank], axis=0)), NT)
    return image_block


STEPS = 8


def cells_first_kernel(x_ref, o_ref, tile_ref, sems):
    step = o_ref.shape[0] // STEPS
    loads = [pltpu.make_async_copy(x_ref.at[:, pl.ds(step * k, step)], tile_ref.at[k], sems.at[k]) for k in range(STEPS)]
    for load in loads:
        load.start()
    for k in range(STEPS):
        loads[k].wait()
        for n in range(step // 128):
            tile = tile_ref[k, :, 128 * n : 128 * (n + 1)].reshape(8, 16, 128)
            rows = jnp.concatenate([tile[:, x, :] for x in range(16)], axis=0)
            at = step * k + 128 * n
            o_ref[at : at + 128, :] = rows.T


def cells_first(block):
    cells = block.shape[2]
    step = cells // STEPS
    return pl.pallas_call(
        cells_first_kernel,
        out_shape=jax.ShapeDtypeStruct((cells, 128), F32),
        in_specs=[pl.BlockSpec(memory_space=pltpu.HBM)],
        out_specs=pl.BlockSpec(memory_space=pltpu.VMEM),
        scratch_shapes=[pltpu.VMEM((STEPS, 128, step), F32), pltpu.SemaphoreType.DMA((STEPS,))],
        compiler_params=grant(50),
    )(block.reshape(128, cells))


def species_gram_kernel(r_ref, o_ref, ht_ref, h_ref, l_ref):
    for s in range(8):
        high, low = split2(r_ref[s])
        ht_ref[128 * s : 128 * (s + 1), :] = high.T
        h_ref[:, 128 * s : 128 * (s + 1)] = high
        l_ref[:, 128 * s : 128 * (s + 1)] = low
    lane = lax.broadcasted_iota(jnp.int32, (8, 256), 1) % 128
    rows = []
    for a in range(4):
        left = ht_ref[256 * a : 256 * (a + 1), :]
        parts = [[], []]
        for b in range(4):
            right = slice(256 * b, 256 * (b + 1))
            prod = bf16_dot(left, l_ref[:, right])
            if b >= a:
                main = bf16_dot(left, h_ref[:, right])
                prod = prod + (main if b > a else 0.5 * main)
            for half in range(2):
                acc = prod[128 * half : 128 * half + 8]
                for x in range(1, 16):
                    acc = jnp.where(lane // 8 == x, prod[128 * half + 8 * x : 128 * half + 8 * x + 8], acc)
                parts[half].append(acc)
        for half in range(2):
            rows.append(jnp.concatenate(parts[half], axis=1))
    wide = jnp.concatenate(rows, axis=0)
    fold = jnp.where(
        lax.broadcasted_iota(jnp.int32, (1024, 64), 0) // 128 * 8
        + lax.broadcasted_iota(jnp.int32, (1024, 64), 0) % 8
        == lax.broadcasted_iota(jnp.int32, (1024, 64), 1),
        1.0,
        0.0,
    ).astype(F32)
    half = exact_dot(wide, fold)
    gram = half + half.T
    second = jnp.concatenate([gram[48:64, 48:64], gram[16:32, 16:64]], axis=1)
    rows = jnp.concatenate([gram[0:16], second, gram[32:48]], axis=0)
    o_ref[...] = jnp.concatenate([rows[0:24], rows[24:48]], axis=1)


def species_gram(received):
    return pl.pallas_call(
        species_gram_kernel,
        out_shape=jax.ShapeDtypeStruct((24, 128), F32),
        scratch_shapes=[
            pltpu.VMEM((1024, 768), BF16),
            pltpu.VMEM((768, 1024), BF16),
            pltpu.VMEM((768, 1024), BF16),
        ],
        compiler_params=grant(16),
    )(received)


def plane_gram_kernel(
    r_ref, g_ref, start_ref, out_ref, mine_ref, other_ref, wh_ref, wl_ref, h_ref, l_ref, red_ref, turned_ref, sem
):
    def between(sweep):
        for s in (2 * sweep, 2 * sweep + 1):
            lanes = slice(128 * s, 128 * (s + 1))
            h_ref[:, lanes], l_ref[:, lanes] = split2(r_ref[s])

    folded = jnp.sum(g_ref[...], axis=0)
    rows = jnp.concatenate([folded[:, 0:64], folded[:, 64:128]], axis=0)
    across_rows = jnp.concatenate(
        [jnp.concatenate([rows, jnp.zeros((80, 64), F32)], axis=0), jnp.zeros((128, 64), F32)], axis=1
    ).T
    second = jnp.concatenate([across_rows[16:32, 0:16], rows[16:32, 16:64]], axis=1)
    last = jnp.concatenate([across_rows[48:64, 0:48], rows[16:32, 0:16]], axis=1)
    gram = jnp.concatenate([rows[0:16], second, rows[32:48], last], axis=0)
    start = jnp.concatenate([start_ref[...], jnp.zeros((112, 64), F32)], axis=0).T
    basis = subspace_narrow(gram, start, between)[:, 0:16]
    column = lax.broadcasted_iota(jnp.int32, (16, 256), 1)
    widen = jnp.where(
        column // 16 % 4 * 4 + column // 64 == lax.broadcasted_iota(jnp.int32, (16, 256), 0), 1.0, 0.0
    ).astype(BF16)
    high, mid, low = split3(basis)
    wide = bf16_dot(jnp.concatenate([high, mid, low], axis=1), jnp.concatenate([widen] * 3, axis=0))
    keep = (
        lax.broadcasted_iota(jnp.int32, (128, 256), 0) // 8 == lax.broadcasted_iota(jnp.int32, (128, 256), 1) % 16
    )
    for s in range(8):
        weights = jnp.where(keep, jnp.concatenate([wide[8 * s : 8 * s + 8]] * 16, axis=0), 0.0)
        high, low = split2(weights)
        wh_ref[128 * s : 128 * (s + 1), :] = high
        wl_ref[128 * s : 128 * (s + 1), :] = low
    wh, wl = wh_ref[...], wl_ref[...]
    for n in range(2):
        rows = slice(384 * n, 384 * (n + 1))
        high = h_ref[rows, :]
        red_ref[rows, :] = bf16_dot(high, wh) + (bf16_dot(high, wl) + bf16_dot(l_ref[rows, :], wh))
    lane = lax.broadcasted_iota(jnp.int32, (24, 128), 1)
    blank = jnp.zeros((8, 128), F32)
    for pair in range(16):
        rows = []
        for k in range(4):
            lanes = slice(128 * (k // 2), 128 * (k // 2 + 1))
            at = 48 * pair
            first, second = red_ref[at : at + 24, lanes], red_ref[at + 24 : at + 48, lanes]
            if k % 2:
                first = pltpu.roll(first, 64, 1)
            else:
                second = pltpu.roll(second, 64, 1)
            rows += [jnp.where(lane < 64, first, second), blank]
        turned = jnp.concatenate(rows, axis=0).T
        for g in range(2):
            for q in range(4):
                at, to = 64 * g + 16 * q, 32 * pair + 16 * g
                turned_ref[to : to + 16, 128 * q : 128 * (q + 1)] = turned[at : at + 16]
    copy = pltpu.make_async_copy(turned_ref, out_ref.at[pl.ds(0, 512)], sem)
    copy.start()
    high, low = split2(turned_ref[...])
    left = jnp.concatenate([high, high, low], axis=1)
    right = jnp.concatenate([high, low, high], axis=1)
    quarter = [slice(0, 256), slice(256, 512)]
    whole = {
        (i, j): bf16_dot(left[quarter[i]], right[quarter[j]], NT) for i, j in ((0, 0), (0, 1), (1, 1))
    }
    blocks = []
    for i in range(4):
        for j in range(i, 4):
            rows, lanes = slice(128 * (i % 2), 128 * (i % 2 + 1)), slice(128 * (j % 2), 128 * (j % 2 + 1))
            blocks.append(whole[i // 2, j // 2][rows, lanes])
    first = lax.axis_index("gx") % 2 == 0
    for n in range(5):
        rows = slice(128 * n, 128 * (n + 1))
        mine_ref[rows, :] = jnp.where(first, blocks[n], blocks[n + 5])
        other_ref[rows, :] = jnp.where(first, blocks[n + 5], blocks[n])
    copy.wait()


def plane_gram(received, grams, start_species):
    half = jax.ShapeDtypeStruct((640, 128), F32)
    whole = pl.BlockSpec(memory_space=pltpu.VMEM)
    return pl.pallas_call(
        plane_gram_kernel,
        out_shape=(jax.ShapeDtypeStruct((SPARE, 512), F32), half, half),
        in_specs=[whole, whole, whole],
        out_specs=(pl.BlockSpec(memory_space=pltpu.HBM), whole, whole),
        scratch_shapes=[
            pltpu.VMEM((1024, 256), BF16),
            pltpu.VMEM((1024, 256), BF16),
            pltpu.VMEM((768, 1024), BF16),
            pltpu.VMEM((768, 1024), BF16),
            pltpu.VMEM((768, 256), F32),
            pltpu.VMEM((512, 512), F32),
            pltpu.SemaphoreType.DMA,
        ],
        compiler_params=grant(20),
    )(received, grams, start_species.T)


def core_kernel(
    mine_ref, other_ref, turned_hbm, start_ref, out_ref, peaks_ref, image_ref, turned_ref, high_ref, low_ref, sem
):
    copy = pltpu.make_async_copy(turned_hbm.at[pl.ds(0, 512)], turned_ref, sem)
    copy.start()
    first = lax.axis_index("gx") % 2 == 0
    blocks = {}
    n = 0
    for i in range(4):
        for j in range(i, 4):
            rows = slice(128 * (n % 5), 128 * (n % 5 + 1))
            mine, other = mine_ref[rows, :], other_ref[rows, :]
            blocks[i, j] = jnp.where(first, mine, other) if n < 5 else jnp.where(first, other, mine)
            if i != j:
                blocks[j, i] = blocks[i, j].T
            n += 1
    gram = jnp.concatenate(
        [jnp.concatenate([blocks[i, j] for j in range(4)], axis=1) for i in range(4)], axis=0
    )

    def aside(sweep, panel):
        if sweep == 1 and panel < 4:
            if panel == 0:
                copy.wait()
            lanes = slice(128 * panel, 128 * (panel + 1))
            high_ref[:, lanes], low_ref[:, lanes] = split2(turned_ref[lanes, :].T)

    basis = subspace(gram, start_ref[...], image_ref, aside)
    bh, bl = split2(basis)
    wide = bf16_dot(high_ref[...], jnp.concatenate([bh, bl], axis=1))
    core = wide[:, 0:128] + (wide[:, 128:256] + bf16_dot(low_ref[...], bh))
    ranks = jnp.concatenate([core[32 * r : 32 * r + 24, :].reshape(1, 24, 128) for r in range(16)], axis=0)
    out_ref[...] = jnp.swapaxes(ranks, 0, 1)
    peaks = jnp.max(jnp.abs(core).reshape(16, 32, 128), axis=2)
    peaks_ref[...] = peaks[:, 0:24]


def core_of(mine, other, turned, start_plane):
    whole = pl.BlockSpec(memory_space=pltpu.VMEM)
    return pl.pallas_call(
        core_kernel,
        out_shape=(jax.ShapeDtypeStruct((24, 16, 128), F32), jax.ShapeDtypeStruct((16, 24), F32)),
        in_specs=[whole, whole, pl.BlockSpec(memory_space=pltpu.HBM), whole],
        scratch_shapes=[
            pltpu.VMEM((512, 128), F32),
            pltpu.VMEM((512, 512), F32),
            pltpu.VMEM((512, 512), BF16),
            pltpu.VMEM((512, 512), BF16),
            pltpu.SemaphoreType.DMA,
        ],
        compiler_params=grant(20),
    )(mine, other, turned, start_plane)


def over_plane(x):
    return lax.all_to_all(x, "gx", 0, 0, tiled=True, axis_index_groups=PLANES)


def copies(x, count):
    return jnp.broadcast_to(x[None], (count,) + x.shape)


def per_device(tensor, start_species, start_plane):
    sent = cells_first(tensor).reshape(256, 24, 128)
    received = lax.all_to_all(sent, BOTH, 0, 0, tiled=True).reshape(8, 768, 128)
    grams = species_gram(received)
    grams = grams + lax.ppermute(grams, "gx", PAIR)
    grams = jnp.sum(lax.all_to_all(copies(grams, 8), "sp", 0, 0, tiled=True), axis=0)
    grams = over_plane(copies(grams, 16))
    turned, mine, other = plane_gram(received, grams, start_species)
    mine = mine + lax.ppermute(other, "gx", PAIR)
    share = jnp.sum(over_plane(mine.reshape(16, 40, 128)), axis=0)
    share = jnp.sum(lax.all_to_all(copies(share, 8), "sp", 0, 0, tiled=True), axis=0)
    mine = over_plane(copies(share, 16)).reshape(640, 128)
    other = lax.ppermute(mine, "gx", PAIR)
    core_block, block_peaks = core_of(mine, other, turned, start_plane)
    return core_block, block_peaks.T


def solution(mesh):
    placed = (P("sp", "gx", None), P(), P())
    return jax.shard_map(
        per_device,
        mesh=mesh,
        in_specs=placed,
        out_specs=(P(BOTH, None, None), P(BOTH, None)),
        check_vma=False,
    )
```
